256 devices in a mesh: rep: 16 (over z_lo, x, core), shard: 16 (over y, z_hi).
Axes of the slice: x: 4, y: 4, z: 8 (z_hi: 4, z_lo: 2; z = z_hi * 2 + z_lo), core: 2. Of those that a mesh axis runs over, the one named last changes fastest.
Arguments:
- acts: bfloat16 [32768, 4096], P(('rep', 'shard')), may hold values from -6 to 6
- out_grad: bfloat16 [32768, 2048], P(('rep', 'shard')), may hold values from -6 to 6
- saved_proj: bfloat16 [32768, 2048], P(('rep', 'shard')), may hold values from -6 to 6
- weight: bfloat16 [4096, 2048], P('shard'), may hold values from -0.09375 to 0.09375
- shift_scale: float32 [64, 2, 4096], replicated, may hold values from -3 to 3
- gate: float32 [64, 2048], replicated, may hold values from -4 to 4
- image_of: int32 [32768], P(('rep', 'shard')), may hold values from 0 to 63, never falling along the last dimension, each value on 1 to 2048 neighbouring positions
Outputs:
- acts_grad: bfloat16 [32768, 4096], P(('rep', 'shard'))
- weight_grad: bfloat16 [4096, 2048], P('shard')
- modulation_grad: float32 [64, 2, 4096], replicated
- gate_grad: float32 [64, 2048], replicated
The draws below stay inside these ranges and needn't reach their ends.
Inputs may be any that keep to these rules, and one draw needn't show every extreme that they name: `image_of`: nondecreasing along the tokens; every image has 1 to 2048 tokens and some image has exactly 2048.
All inputs are finite; a program needn't handle non-finite values.
Results may differ from the reference program's by a relative error of at most 0.0057.
Values may be sent and summed in bfloat16 or wider, within the bound.
A program may use at most 128 MiB of HBM per device.

```python
import math
import jax
import jax.numpy as jnp
import numpy as np
from jax import lax

D = 4096
DH = 2048
MEAN_IMG = 512
TOKENS = 32768
IMAGES = 64
MOST_IMG = 2048


def level_of(stream_key, shape, shards, smallest, high):
    loudness = 1.0
    for dim, parts in shards:
        heights = jax.random.uniform(jax.random.fold_in(jax.random.fold_in(stream_key, 6), dim), (parts,), jnp.float32, smallest / len(shards), high / len(shards))
        loudness = loudness * jnp.repeat(jnp.exp(heights), shape[dim] // parts).reshape((-1,) + (1,) * (len(shape) - 1 - dim))
    return loudness


def length_profile(count, total, bound, lean):
    loads = [(1 << 20) // math.isqrt(standing ** lean) + 1 for standing in range(2, count + 1)]
    spare, given = total - bound - (count - 1), [1] * (count - 1)
    while spare > 0:
        movable = [i for i in range(count - 1) if given[i] < bound]
        mass, remaining = sum([loads[i] for i in movable]), spare
        for i in movable:
            addition = min(bound - given[i], max(1, remaining * loads[i] // mass), spare)
            given[i] = given[i] + addition
            spare = spare - addition
    return np.array([bound] + given)


def uneven_parts(key, amount, total, most, slope):
    if amount == 2:
        one = jax.random.randint(key, (), max(1, total - most), min(most, total - 1) + 1)
        return jnp.stack([one, total - one])
    tallies = jnp.asarray(length_profile(amount, total, most, slope), jnp.int32)
    twos = (amount - 1) // 2
    donor, sink = tallies[1:1 + 2 * twos:2], tallies[2:2 + 2 * twos:2]
    room = jnp.minimum(donor - 1, most - sink)
    passed = jax.random.randint(jax.random.fold_in(key, 1), (twos,), 0, 1 << 20) % (room + 1)
    tallies = tallies.at[1:1 + 2 * twos:2].set(donor - passed).at[2:2 + 2 * twos:2].set(sink + passed)
    return tallies[jax.random.permutation(jax.random.fold_in(key, 2), amount)]


def bell_draw(stream_key, extent, width, reach, shards=(), kind=jnp.bfloat16):
    result = width * jax.random.normal(stream_key, extent, jnp.float32)
    if shards:
        result = result * level_of(stream_key, extent, shards, -0.22, 0.18)
    return jnp.clip(result, -reach, reach).astype(kind)


def setup_inputs(seed: int = 0) -> dict:
    keys = jax.random.split(jax.random.key(seed), 8)
    acts = bell_draw(keys[0], (TOKENS, D), 1.0, 6.0, ((0, 256),))
    out_grad = bell_draw(keys[1], (TOKENS, DH), 1.0, 6.0, ((0, 256),))
    saved_proj = bell_draw(keys[2], (TOKENS, DH), 1.0, 6.0, ((0, 256),))
    weight = bell_draw(keys[3], (D, DH), D ** -0.5, 0.09375, ((0, 16),))
    shift_scale = bell_draw(keys[4], (IMAGES, 2, D), 0.5, 3.0, (), jnp.float32)
    gate = bell_draw(keys[5], (IMAGES, DH), 1.0, 4.0, (), jnp.float32)
    image_of = jnp.searchsorted(jnp.cumsum(uneven_parts(keys[6], IMAGES, TOKENS, MOST_IMG, 2)), jnp.arange(TOKENS), side="right").astype(jnp.int32)
    return dict(acts=acts, out_grad=out_grad, saved_proj=saved_proj, weight=weight, shift_scale=shift_scale, gate=gate, image_of=image_of)


def reference(acts, out_grad, saved_proj, weight, shift_scale, gate, image_of):
    values = acts.astype(jnp.float32)
    center = values - lax.optimization_barrier(jnp.mean(values, axis=1, keepdims=True))
    recip = lax.rsqrt(lax.optimization_barrier(jnp.mean(center * center, axis=1, keepdims=True)) + 1e-06)
    normed = center * recip
    shift_rows = shift_scale[:, 0][image_of]
    scale_rows = shift_scale[:, 1][image_of]
    gate_rows = gate[image_of]
    hidden = (normed * (1.0 + scale_rows) + shift_rows).astype(jnp.bfloat16)
    grad_flat = out_grad.astype(jnp.float32)
    dz = (gate_rows * grad_flat).astype(jnp.bfloat16)
    weight_grad = lax.dot_general(hidden, dz, (((0,), (0,)), ((), ())), preferred_element_type=jnp.float32)
    weight_grad = (weight_grad * TOKENS ** (-0.5)).astype(jnp.bfloat16)
    dh = lax.dot_general(dz, weight, (((1,), (1,)), ((), ())), preferred_element_type=jnp.float32)
    dnorm = dh * (1.0 + scale_rows)
    acts_grad = recip * (dnorm - lax.optimization_barrier(jnp.mean(dnorm, axis=1, keepdims=True)) - normed * lax.optimization_barrier(jnp.mean(dnorm * normed, axis=1, keepdims=True)))
    factor = MEAN_IMG ** (-0.5)
    shift_grad = jax.ops.segment_sum(dh, image_of, IMAGES) * factor
    scale_grad = jax.ops.segment_sum(dh * normed, image_of, IMAGES) * factor
    gate_grad = jax.ops.segment_sum(grad_flat * saved_proj.astype(jnp.float32), image_of, IMAGES) * factor
    return (acts_grad.astype(jnp.bfloat16), weight_grad, jnp.stack([shift_grad, scale_grad], axis=1), gate_grad)
```

```python
import jax
import jax.numpy as jnp
from jax import lax
from jax.experimental import pallas as pl
from jax.experimental.pallas import tpu as pltpu
from jax.sharding import PartitionSpec as P

MEAN_IMG = 512
MESH = pl.DeviceIdType.MESH
BF16 = jnp.bfloat16
F32 = jnp.float32
CHUNKS = (
    (0, 384, (0, 1, 2)),
    (384, 384, (1, 2, 0)),
    (768, 256, (2, 0, 1)),
    (1024, 256, (0, 1, 2)),
    (1280, 384, (1, 2, 0)),
    (1664, 384, (2, 0, 1)),
)


def place():
    r = lax.axis_index("rep")
    s = lax.axis_index("shard")
    return (r // 2) % 4, s // 4, (s % 4) * 2 + r // 8, r % 2


def dev(x, y, z, c):
    return ((z % 2) * 8 + x * 2 + c, y * 4 + z // 2)


def band_of(x, y, z, c):
    zb, zh = z % 2, z // 2
    p = (x + c) % 2
    e = (zb + zh) % 2
    step = c * (2 * zb + 3) + (1 - c) * 2 * (1 - e)
    return y + p * (3 - 2 * y), (zh + step) % 4


def flip(pos, bits):
    x, y, z, c = pos
    if bits & 1:
        x = x + 1 - 2 * (x % 2)
    if bits & 2:
        y = y + 1 - 2 * (y % 2)
    if bits & 4:
        z = z + 1 - 2 * (z % 2)
    if bits & 8:
        c = 1 - c
    return x, y, z, c


def cube_index(pos):
    x, y, z, c = pos
    return x % 2 + 2 * (y % 2) + 4 * (z % 2) + 8 * c


def twin(cube, yp, zh):
    cx, cy, cz = cube
    d = (zh - cz + 4) % 4
    c = d % 2
    zb = c * ((3 - d) // 2) + (1 - c) * ((1 + d // 2 + cz) % 2)
    q = (yp // 2 + cy) % 2
    y = yp + q * (3 - 2 * yp)
    return 2 * cx + (q + c) % 2, y, 2 * cz + zb, c


def signal(pos):
    pl.semaphore_signal(
        pltpu.get_barrier_semaphore(), inc=1, device_id=dev(*pos), device_id_type=MESH
    )


def remote(src, dst, ss, rs, pos):
    return pltpu.make_async_remote_copy(
        src_ref=src,
        dst_ref=dst,
        send_sem=ss,
        recv_sem=rs,
        device_id=dev(*pos),
        device_id_type=MESH,
    )


def gather_kernel(
    dz, nrm, gm, w, dz_all, nrm_b, gm_b, w_b,
    dz_s, dz_r, core_s, core_r, nrm_s, nrm_r, gm_s, gm_r, w_s, w_r, loc,
):
    me = place()
    x, y, z, c = me
    zb, zh = z % 2, z // 2
    g = cube_index(me)
    p = (x + c) % 2
    e = (zb + zh) % 2
    yc = y + p * (3 - 2 * y)
    far = (x, yc, (z + (2 * zb - 1) * (3 - 2 * c) + 8) % 8, c)
    near = (x, 3 - y, z, c)
    keeps = (1 - c) * e * (1 - p)
    swaps = (1 - c) * e * p
    sends_far = c + (1 - c) * e

    for k in range(1, 16):
        signal(flip(me, k))
    signal(far)

    @pl.when(swaps == 1)
    def _():
        signal(near)

    pl.semaphore_wait(pltpu.get_barrier_semaphore(), 16 + swaps)

    own = pltpu.make_async_copy(dz, dz_all.at[g], loc.at[0])
    own.start()
    bx, by = band_of(*me)
    own_nrm = pltpu.make_async_copy(
        nrm.at[:, pl.ds(pl.multiple_of((bx * 4 + by) * 256, 256), 256)], nrm_b.at[g], loc.at[1]
    )
    own_nrm.start()
    own_gm = pltpu.make_async_copy(gm.at[bx * 4 + by], gm_b.at[g], loc.at[2])
    own_gm.start()

    copies = {}
    for n, (at, width, order) in enumerate(CHUNKS):
        cols = pl.ds(at, width)
        cp = remote(
            dz.at[:, cols], dz_all.at[g, :, cols], dz_s.at[n, 0], dz_r.at[n, 0],
            flip(me, 1 << order[0]),
        )
        cp.start()
        copies[n, 0] = cp

    to_far = remote(w, w_b, w_s.at[0], w_r, far)
    to_near = remote(w, w_b, w_s.at[1], w_r, near)
    to_self = pltpu.make_async_copy(w, w_b, w_r)

    @pl.when(sends_far == 1)
    def _():
        to_far.start()

    @pl.when(swaps == 1)
    def _():
        to_near.start()

    @pl.when(keeps == 1)
    def _():
        to_self.start()

    small = []
    for k in range(1, 16):
        to = flip(me, k)
        by, bz = band_of(*to)
        b = by * 4 + bz
        cp = remote(
            nrm.at[:, pl.ds(pl.multiple_of(b * 256, 256), 256)], nrm_b.at[g],
            nrm_s.at[k], nrm_r.at[k], to,
        )
        cp.start()
        small.append(cp)
        cp = remote(gm.at[b], gm_b.at[g], gm_s.at[k], gm_r.at[k], to)
        cp.start()
        small.append(cp)

    for n, (at, width, order) in enumerate(CHUNKS):
        cols = pl.ds(at, width)
        one = flip(me, 1 << order[0])
        to = flip(me, 1 << order[1])
        cp = remote(
            dz.at[:, cols], dz_all.at[g, :, cols], dz_s.at[n, 1], dz_r.at[n, 1], to
        )
        cp.start()
        copies[n, 1] = cp
        copies[n, 0].wait_recv()
        slot = dz_all.at[cube_index(one), :, cols]
        cp = remote(slot, slot, dz_s.at[n, 2], dz_r.at[n, 2], to)
        cp.start()
        copies[n, 2] = cp
    for n, (at, width, order) in enumerate(CHUNKS):
        cols = pl.ds(at, width)
        to = flip(me, 1 << order[2])
        cp = remote(
            dz.at[:, cols], dz_all.at[g, :, cols], dz_s.at[n, 3], dz_r.at[n, 3], to
        )
        cp.start()
        copies[n, 3] = cp
        for j, bits in (
            (4, 1 << order[0]),
            (5, 1 << order[1]),
            (6, (1 << order[0]) + (1 << order[1])),
        ):
            if j > 4:
                copies[n, j - 4].wait_recv()
            slot = dz_all.at[cube_index(flip(me, bits)), :, cols]
            cp = remote(slot, slot, dz_s.at[n, j], dz_r.at[n, j], to)
            cp.start()
            copies[n, j] = cp
    own.wait()
    for n, (at, width, order) in enumerate(CHUNKS):
        for j in range(3, 7):
            copies[n, j].wait_recv()
        half = dz_all.at[pl.ds(c * 8, 8), :, pl.ds(at, width)]
        cp = remote(half, half, core_s.at[n], core_r.at[n], flip(me, 8))
        cp.start()
        copies[n, 7] = cp
    for n in range(len(CHUNKS)):
        for j in range(7):
            copies[n, j].wait_send()
        copies[n, 7].wait()
    for cp in small:
        cp.wait()
    own_nrm.wait()
    own_gm.wait()
    to_far.wait_recv()

    @pl.when(sends_far == 1)
    def _():
        to_far.wait_send()

    @pl.when(swaps == 1)
    def _():
        to_near.wait_send()


def gather(dz, nrm, gm, w):
    rows, wide = dz.shape
    n = len(CHUNKS)
    dma = pltpu.SemaphoreType.DMA
    hbm = pl.BlockSpec(memory_space=pl.ANY)
    return pl.pallas_call(
        gather_kernel,
        out_shape=(
            jax.ShapeDtypeStruct((16, rows, wide), BF16),
            jax.ShapeDtypeStruct((16, rows, 256), BF16),
            jax.ShapeDtypeStruct((16, 80, 128), BF16),
            jax.ShapeDtypeStruct(w.shape, BF16),
        ),
        in_specs=[hbm] * 4,
        out_specs=[hbm] * 4,
        scratch_shapes=[
            dma((n, 7)), dma((n, 7)), dma((n,)), dma((n,)),
            dma((16,)), dma((16,)), dma((16,)), dma((16,)),
            dma((2,)), dma, dma((3,)),
        ],
        compiler_params=pltpu.CompilerParams(collective_id=0, has_side_effects=True),
        name="gather_cube",
    )(dz, nrm, gm, w)


def exchange_kernel(dh, msg, dh_full, parts, dh_s, dh_r, ms_s, ms_r, loc):
    me = place()
    x, y, z, c = me
    zb, zh = z % 2, z // 2
    g = cube_index(me)
    by, bz = band_of(*me)
    b = by * 4 + bz
    mine = (1 - c) * ((zb + zh) % 2) * (1 - (x + c) % 2)
    q = x // 2 + 2 * (y // 2) + 4 * zh

    for k in range(1, 16):
        signal(flip(me, k))
    for k in range(16):
        cube = ((x // 2 + k % 2) % 2, (y // 2 + k // 2 % 2) % 2, (zh + k // 4) % 4)
        if k == 0:

            @pl.when(mine == 0)
            def _():
                signal(twin(cube, y, zh))

        else:
            signal(twin(cube, y, zh))
    pl.semaphore_wait(pltpu.get_barrier_semaphore(), 31 - mine)

    own = pltpu.make_async_copy(
        dh.at[g], dh_full.at[:, pl.ds(pl.multiple_of(b * 256, 256), 256)], loc.at[0]
    )
    own.start()
    sends, first = [], None
    for k in range(16):
        hx, hl, hc = (x + k % 4) % 4, (zb + k // 4 % 2) % 2, (c + k // 8) % 2
        piece = msg.at[hx + 4 * hl + 8 * hc]
        to = (hx, by, 2 * bz + hl, hc)
        cp = remote(piece, parts.at[q], ms_s.at[k], ms_r.at[q], to)
        if k == 0:
            first = cp
            keep = pltpu.make_async_copy(piece, parts.at[q], ms_r.at[q])

            @pl.when(mine == 0)
            def _():
                first.start()

            @pl.when(mine == 1)
            def _():
                keep.start()

        else:
            cp.start()
            sends.append(cp)
    blocks = []
    for k in range(1, 16):
        to = flip(me, k)
        cp = remote(
            dh.at[cube_index(to)],
            dh_full.at[:, pl.ds(pl.multiple_of(b * 256, 256), 256)],
            dh_s.at[k], dh_r.at[k], to,
        )
        cp.start()
        blocks.append(cp)
    own.wait()
    for cp in blocks:
        cp.wait()
    for cp in sends:
        cp.wait_send()

    @pl.when(mine == 0)
    def _():
        first.wait_send()

    for k in range(16):
        pltpu.make_async_copy(parts.at[k], parts.at[k], ms_r.at[k]).wait()


def exchange(dh, msg):
    dma = pltpu.SemaphoreType.DMA
    hbm = pl.BlockSpec(memory_space=pl.ANY)
    return pl.pallas_call(
        exchange_kernel,
        out_shape=(
            jax.ShapeDtypeStruct((dh.shape[1], 4096), BF16),
            jax.ShapeDtypeStruct(msg.shape, BF16),
        ),
        in_specs=[hbm] * 2,
        out_specs=[hbm] * 2,
        scratch_shapes=[
            dma((16,)), dma((16,)), dma((16,)), dma((16,)), dma((1,)),
        ],
        compiler_params=pltpu.CompilerParams(collective_id=1, has_side_effects=True),
        name="exchange_parts",
    )(dh, msg)


def spread_kernel(wp, s, w_all, s_all, s1_s, s1_r, w_s, w_r, s2_s, s2_r, co_s, co_r, loc):
    me = place()
    x, y, z, c = me
    zb, zh = z % 2, z // 2
    h = x + 4 * zb + 8 * c
    sib = flip(me, 8)
    plane = [(x, (y + k // 4) % 4, (2 * (zh + k % 4)) % 8 + zb, c) for k in range(1, 16)]
    line = [((x + k % 4) % 4, y, 2 * zh + (zb + k // 4) % 2, c) for k in range(1, 8)]
    for to in plane + line + [sib]:
        signal(to)
    pl.semaphore_wait(pltpu.get_barrier_semaphore(), 23)

    b = y * 4 + zh
    own_s = pltpu.make_async_copy(s, s_all.at[h, b], loc.at[0])
    own_w = pltpu.make_async_copy(wp, w_all.at[h], loc.at[1])
    own_s.start()
    own_w.start()
    firsts = []
    for k, to in enumerate(plane):
        cp = remote(s, s_all.at[h, b], s1_s.at[k], s1_r.at[k], to)
        cp.start()
        firsts.append(cp)
    rest = []
    for k, to in enumerate(line):
        cp = remote(wp, w_all.at[h], w_s.at[k], w_r.at[k], to)
        cp.start()
        rest.append(cp)
    own_s.wait()
    for cp in firsts:
        cp.wait_recv()
    for k, to in enumerate(line):
        cp = remote(s_all.at[h], s_all.at[h], s2_s.at[k], s2_r.at[k], to)
        cp.start()
        rest.append(cp)
    own_w.wait()
    for cp in rest:
        cp.wait_recv()
    half = pl.ds(c * 8, 8)
    last = [
        remote(w_all.at[half], w_all.at[half], co_s.at[0], co_r.at[0], sib),
        remote(s_all.at[half], s_all.at[half], co_s.at[1], co_r.at[1], sib),
    ]
    for cp in last:
        cp.start()
    for cp in firsts + rest:
        cp.wait_send()
    for cp in last:
        cp.wait()


def spread(wp, s):
    dma = pltpu.SemaphoreType.DMA
    hbm = pl.BlockSpec(memory_space=pl.ANY)
    return pl.pallas_call(
        spread_kernel,
        out_shape=(
            jax.ShapeDtypeStruct((16,) + wp.shape, BF16),
            jax.ShapeDtypeStruct((16, 16) + s.shape, BF16),
        ),
        in_specs=[hbm] * 2,
        out_specs=[hbm] * 2,
        scratch_shapes=[
            dma((15,)), dma((15,)), dma((7,)), dma((7,)),
            dma((7,)), dma((7,)), dma((2,)), dma((2,)), dma((2,)),
        ],
        compiler_params=pltpu.CompilerParams(collective_id=2, has_side_effects=True),
        name="spread_sums",
    )(wp, s)


def split_dot(onehot, table):
    hi = table.astype(BF16)
    lo = (table - hi.astype(F32)).astype(BF16)
    dims = (((0,), (0,)), ((), ()))
    return lax.dot_general(onehot, hi, dims, preferred_element_type=F32) + lax.dot_general(
        onehot, lo, dims, preferred_element_type=F32
    )


def on_device(acts, out_grad, saved_proj, weight, shift_scale, gate, image_of):
    rows = acts.shape[0]
    images = gate.shape[0]
    total = rows * lax.axis_size("shard") * lax.axis_size("rep")
    values = acts.astype(F32)
    center = values - jnp.mean(values, axis=1, keepdims=True)
    recip = lax.rsqrt(jnp.mean(center * center, axis=1, keepdims=True) + 1e-06)
    normed = center * recip
    numbers = jnp.arange(images, dtype=jnp.int32)[:, None]
    onehot = (image_of[None, :] == numbers).astype(BF16)
    grad_flat = out_grad.astype(F32)
    dz = (split_dot(onehot, gate) * grad_flat).astype(BF16)
    gate_part = jnp.dot(
        onehot.astype(F32),
        grad_flat * saved_proj.astype(F32),
        precision=lax.Precision.HIGHEST,
    )
    gm = gate_part.astype(BF16).reshape(images, 16, 128).transpose(1, 0, 2)
    ids = jnp.broadcast_to(image_of.astype(BF16)[None, None, :], (16, 16, 128))
    gm = jnp.concatenate([gm, ids], axis=1)
    dz_all, nrm_b, gm_b, w_b = gather(dz, normed.astype(BF16), gm, weight)

    by, bz = band_of(*place())
    band = by * 4 + bz
    dz_all = dz_all.reshape(16 * rows, -1)
    nrm_b = nrm_b.reshape(16 * rows, 256)
    cube_ids = gm_b[:, images, :].reshape(1, 16 * rows)
    cube_hot = (cube_ids == numbers.astype(BF16)).astype(BF16)
    table = lax.dynamic_slice_in_dim(shift_scale, band * 256, 256, axis=2).reshape(images, 512)
    mods = split_dot(cube_hot, table)
    nrm_f = nrm_b.astype(F32)
    hidden = (nrm_f * (1.0 + mods[:, 256:]) + mods[:, :256]).astype(BF16)
    wg = lax.dot_general(
        hidden, dz_all, (((0,), (0,)), ((), ())), preferred_element_type=F32
    ).astype(BF16)
    dh = lax.dot_general(dz_all, w_b, (((1,), (1,)), ((), ())), preferred_element_type=F32)
    both = jnp.concatenate([dh, dh * nrm_f], axis=1)
    hi = both.astype(BF16)
    lo = (both - hi.astype(F32)).astype(BF16)
    sums = jnp.dot(cube_hot, hi, preferred_element_type=F32) + jnp.dot(
        cube_hot, lo, preferred_element_type=F32
    )
    gate_sum = jnp.sum(gm_b[:, :images, :].astype(F32), axis=0)
    mod_piece = sums.astype(BF16).reshape(16, 16, 128)
    gate_piece = jnp.pad(gate_sum.astype(BF16).reshape(16, 4, 128), ((0, 0), (0, 12), (0, 0)))
    msg = jnp.concatenate([wg.reshape(16, 16, -1), mod_piece, gate_piece], axis=2)
    dh_full, parts = exchange(dh.astype(BF16).reshape(16, rows, 256), msg)

    red = jnp.sum(parts.astype(F32), axis=0)
    wp = (red[:, :2048] * total ** (-0.5)).astype(BF16)
    s = (red[:, 2048:] * MEAN_IMG ** (-0.5)).astype(BF16)
    w_all, s_all = spread(wp, s)

    scale_rows = split_dot(onehot, shift_scale[:, 1])
    dnorm = dh_full.astype(F32) * (1.0 + scale_rows)
    acts_grad = recip * (
        dnorm
        - jnp.mean(dnorm, axis=1, keepdims=True)
        - normed * jnp.mean(dnorm * normed, axis=1, keepdims=True)
    )
    mod = s_all[..., :128].reshape(16, 16, 4, 2, 2, 128).transpose(0, 2, 3, 1, 4, 5)
    modulation_grad = mod.reshape(images, 2, -1).astype(F32)
    gate_grad = s_all[:, :, :4, 128:].transpose(0, 2, 1, 3).reshape(images, -1).astype(F32)
    return (
        acts_grad.astype(BF16),
        w_all.reshape(256, -1),
        modulation_grad,
        gate_grad,
    )


def solution(mesh):
    placed = (
        P(("rep", "shard"), None),
        P(("rep", "shard"), None),
        P(("rep", "shard"), None),
        P("shard", None),
        P(),
        P(),
        P(("rep", "shard")),
    )
    return jax.shard_map(
        on_device,
        mesh=mesh,
        in_specs=placed,
        out_specs=(P(("rep", "shard"), None), P("shard", None), P(), P()),
        check_vma=False,
    )
```

```python
import jax
import jax.numpy as jnp
from jax import lax
from jax.experimental import pallas as pl
from jax.experimental.pallas import tpu as pltpu
from jax.sharding import PartitionSpec as P

MEAN_IMG = 512
MESH = pl.DeviceIdType.MESH
BF16 = jnp.bfloat16
F32 = jnp.float32
CHUNKS = (
    (0, 384, (0, 1, 2)),
    (384, 384, (1, 2, 0)),
    (768, 256, (2, 0, 1)),
    (1024, 256, (0, 1, 2)),
    (1280, 384, (1, 2, 0)),
    (1664, 384, (2, 0, 1)),
)


def place():
    r = lax.axis_index("rep")
    s = lax.axis_index("shard")
    return (r // 2) % 4, s // 4, (s % 4) * 2 + r // 8, r % 2


def dev(x, y, z, c):
    return ((z % 2) * 8 + x * 2 + c, y * 4 + z // 2)


def band_of(x, y, z, c):
    zb, zh = z % 2, z // 2
    p = (x + c) % 2
    e = (zb + zh) % 2
    step = c * (2 * zb + 3) + (1 - c) * 2 * (1 - e)
    return y + p * (3 - 2 * y), (zh + step) % 4


def flip(pos, bits):
    x, y, z, c = pos
    if bits & 1:
        x = x + 1 - 2 * (x % 2)
    if bits & 2:
        y = y + 1 - 2 * (y % 2)
    if bits & 4:
        z = z + 1 - 2 * (z % 2)
    if bits & 8:
        c = 1 - c
    return x, y, z, c


def cube_index(pos):
    x, y, z, c = pos
    return x % 2 + 2 * (y % 2) + 4 * (z % 2) + 8 * c


def twin(cube, yp, zh):
    cx, cy, cz = cube
    d = (zh - cz + 4) % 4
    c = d % 2
    zb = c * ((3 - d) // 2) + (1 - c) * ((1 + d // 2 + cz) % 2)
    q = (yp // 2 + cy) % 2
    y = yp + q * (3 - 2 * yp)
    return 2 * cx + (q + c) % 2, y, 2 * cz + zb, c


def signal(pos):
    pl.semaphore_signal(
        pltpu.get_barrier_semaphore(), inc=1, device_id=dev(*pos), device_id_type=MESH
    )


def remote(src, dst, ss, rs, pos):
    return pltpu.make_async_remote_copy(
        src_ref=src,
        dst_ref=dst,
        send_sem=ss,
        recv_sem=rs,
        device_id=dev(*pos),
        device_id_type=MESH,
    )


def dot(a, b, dims):
    return lax.dot_general(a, b, (dims, ((), ())), preferred_element_type=F32)


def two_terms(v):
    hi = v.astype(BF16)
    return hi, (v - hi.astype(F32)).astype(BF16)


def image_hot(ids, count):
    rows = lax.broadcasted_iota(jnp.int32, (count, ids.shape[1]), 0).astype(F32)
    return jnp.where(rows == ids, 1.0, 0.0)


def block_kernel(
    acts, og, sp, w, ss, gate, ids,
    o_acts, o_w, o_mod, o_gate,
    acts_v, og_v, sp_v, gate_v, ss_v, ss_b, rm, st, dz_all, acts_b, st_b, gm, gm_b, w_b,
    hid, nrm, dh, dh_b, msg_w, msg_s, part_w, part_s, dh_full, sc1, wp, s_own, s1, s_mod, gd,
    o2, v2,
    dz_s, dz_r, core_s, core_r, ac_s, ac_r, st_s, st_r, gm_s, gm_r, w_s, w_r,
    dh_s, dh_r, mw_s, mw_r, ms_s, ms_r, s1_s, s1_r, wp_s, wp_r, sm_s, sm_r, gd_s, gd_r,
    co_s, co_r, loc,
):
    me = place()
    x, y, z, c = me
    zb, zh = z % 2, z // 2
    g = cube_index(me)
    p = (x + c) % 2
    e = (zb + zh) % 2
    far = (x, y + p * (3 - 2 * y), (z + (2 * zb - 1) * (3 - 2 * c) + 8) % 8, c)
    near = (x, 3 - y, z, c)
    keeps = (1 - c) * e * (1 - p)
    swaps = (1 - c) * e * p
    sends_far = c + (1 - c) * e
    by, bz = band_of(*me)
    b = by * 4 + bz
    mine = keeps
    q = x // 2 + 2 * (y // 2) + 4 * zh
    h = x + 4 * zb + 8 * c
    kept = y * 4 + zh
    sib = flip(me, 8)
    plane = [(x, (y + k // 4) % 4, (2 * (zh + k % 4)) % 8 + zb, c) for k in range(1, 16)]
    line = [((x + k % 4) % 4, y, 2 * zh + (zb + k // 4) % 2, c) for k in range(1, 8)]
    band_cols = pl.ds(pl.multiple_of(b * 256, 256), 256)

    loads = [
        pltpu.make_async_copy(a, v, loc.at[i])
        for i, (a, v) in enumerate(
            ((og, og_v), (gate, gate_v), (acts, acts_v), (sp, sp_v),
             (ss.at[:, :, band_cols], ss_b), (ss, ss_v), (acts.at[:, band_cols], acts_b.at[g]))
        )
    ]
    for cp in loads:
        cp.start()
    for k in range(1, 16):
        signal(flip(me, k))
    signal(far)

    @pl.when(swaps == 1)
    def _():
        signal(near)

    for k in range(16):
        cube = ((x // 2 + k % 2) % 2, (y // 2 + k // 2 % 2) % 2, (zh + k // 4) % 4)
        if k == 0:

            @pl.when(mine == 0)
            def _():
                signal(twin(cube, y, zh))

        else:
            signal(twin(cube, y, zh))
    for to in plane + line:
        signal(to)

    ids_f = ids[...].astype(F32)
    hot = image_hot(ids_f, 128)
    hot_t = hot.T[:, :64].astype(BF16)
    loads[0].wait()
    loads[1].wait()
    for j in range(0, 2048, 512):
        cols = slice(j, j + 512)
        hi, lo = two_terms(gate_v[:, cols])
        rows = dot(hot_t, hi, ((1,), (0,))) + dot(hot_t, lo, ((1,), (0,)))
        dz_all[g, :, cols] = (rows * og_v[:, cols].astype(F32)).astype(BF16)

    pl.semaphore_wait(pltpu.get_barrier_semaphore(), 54 + swaps - mine)

    copies = {}

    def relay(n, j, bits, to):
        at, width, _ = CHUNKS[n]
        slot = dz_all.at[cube_index(flip(me, bits)), :, pl.ds(at, width)]
        cp = remote(slot, slot, dz_s.at[n, j], dz_r.at[n, j], to)
        cp.start()
        copies[n, j] = cp

    for n, (_, _, order) in enumerate(CHUNKS):
        relay(n, 0, 0, flip(me, 1 << order[0]))

    to_far = remote(w, w_b, w_s.at[0], w_r, far)
    to_near = remote(w, w_b, w_s.at[1], w_r, near)
    to_self = pltpu.make_async_copy(w, w_b, w_r)

    @pl.when(sends_far == 1)
    def _():
        to_far.start()

    @pl.when(swaps == 1)
    def _():
        to_near.start()

    @pl.when(keeps == 1)
    def _():
        to_self.start()

    loads[2].wait()

    def stats(i, _):
        rows = pl.ds(pl.multiple_of(i * 16, 16), 16)
        v = acts_v[rows, :].astype(F32)
        m = jnp.mean(v, axis=1, keepdims=True)
        v = v - m
        r = lax.rsqrt(jnp.mean(v * v, axis=1, keepdims=True) + 1e-06)
        lane = lax.broadcasted_iota(jnp.int32, (16, 128), 1)
        rm[rows, :] = jnp.where(lane == 0, r, jnp.where(lane == 1, m, 0.0))
        return 0

    lax.fori_loop(0, 8, stats, 0)
    turned = rm[...].T[:8, :]
    row = lax.broadcasted_iota(jnp.int32, (8, 128), 0)
    st[...] = jnp.where(row == 2, ids_f, turned)
    st_b[g] = st[...]

    for n, (_, _, order) in enumerate(CHUNKS):
        to = flip(me, 1 << order[1])
        relay(n, 1, 0, to)
        copies[n, 0].wait_recv()
        relay(n, 2, 1 << order[0], to)

    blocks = []
    for k in range(1, 16):
        to = flip(me, k)
        ty, tz = band_of(*to)
        cols = pl.ds(pl.multiple_of((ty * 4 + tz) * 256, 256), 256)
        blocks.append(remote(st, st_b.at[g], st_s.at[k], st_r.at[k], to))
        blocks.append(remote(acts.at[:, cols], acts_b.at[g], ac_s.at[k], ac_r.at[k], to))
    for cp in blocks:
        cp.start()

    for n, (_, _, order) in enumerate(CHUNKS):
        to = flip(me, 1 << order[2])
        one, two = 1 << order[0], 1 << order[1]
        relay(n, 3, 0, to)
        relay(n, 4, one, to)
        copies[n, 1].wait_recv()
        relay(n, 5, two, to)
        copies[n, 2].wait_recv()
        relay(n, 6, one + two, to)

    loads[3].wait()
    hot_b = hot[:64].astype(BF16)
    for j in range(0, 2048, 512):
        cols = slice(j, j + 512)
        hi, lo = two_terms(og_v[:, cols].astype(F32) * sp_v[:, cols].astype(F32))
        gm[:, cols] = (dot(hot_b, hi, ((1,), (0,))) + dot(hot_b, lo, ((1,), (0,)))).astype(BF16)
    gm_b[g] = gm[:, pl.ds(pl.multiple_of(b * 128, 128), 128)]
    gates = []
    for k in range(1, 16):
        to = flip(me, k)
        ty, tz = band_of(*to)
        cols = pl.ds(pl.multiple_of((ty * 4 + tz) * 128, 128), 128)
        cp = remote(gm.at[:, cols], gm_b.at[g], gm_s.at[k], gm_r.at[k], to)
        cp.start()
        gates.append(cp)

    loads[5].wait()

    def scales(j, _):
        cols = pl.ds(pl.multiple_of(j * 512, 512), 512)
        hi, lo = two_terms(ss_v[:, 1, cols])
        sc1[:, cols] = 1.0 + (dot(hot_t, hi, ((1,), (0,))) + dot(hot_t, lo, ((1,), (0,))))
        return 0

    lax.fori_loop(0, 8, scales, 0)

    loads[4].wait()
    loads[6].wait()
    for cp in blocks:
        cp.wait_recv()
    shift_hi, shift_lo = two_terms(ss_b[:, 0, :])
    scale_hi, scale_lo = two_terms(ss_b[:, 1, :])
    tables = jnp.concatenate(
        [
            jnp.concatenate([shift_hi, scale_hi], axis=1),
            jnp.concatenate([shift_lo, scale_lo], axis=1),
        ],
        axis=0,
    )

    def modulate(t, _):
        block = st_b[t]
        wide = jnp.concatenate([block, jnp.zeros((120, 128), F32)], axis=0).T
        r, m = wide[:, 0:1], wide[:, 1:2]
        own = image_hot(block[2:3], 64)
        twice = jnp.concatenate([own, own], axis=0).T.astype(BF16)
        mods = dot(twice, tables, ((1,), (0,)))
        normed = (acts_b[t].astype(F32) - m) * r
        nrm[t] = normed
        out = normed * (1.0 + mods[:, 256:]) + mods[:, :256]
        hid[:, pl.ds(pl.multiple_of(t * 128, 128), 128)] = out.T.astype(BF16)
        rows = lax.broadcasted_iota(jnp.int32, (128, 128), 0)
        hit = ((rows // 2).astype(F32) == block[2:3])
        o2[:, pl.ds(pl.multiple_of(t * 128, 128), 128)] = jnp.where(
            hit & (rows % 2 == 0), 1.0, 0.0
        ).astype(BF16)
        o2[:, pl.ds(pl.multiple_of(2048 + t * 128, 128), 128)] = jnp.where(
            hit & (rows % 2 == 1), 1.0, 0.0
        ).astype(BF16)
        return 0

    lax.fori_loop(0, 16, modulate, 0)

    parts, first = [], []
    for half in range(2):
        for n in range(3 * half, 3 * half + 3):
            at, width, _ = CHUNKS[n]
            for j in range(3, 7):
                copies[n, j].wait_recv()
            slots = dz_all.at[pl.ds(c * 8, 8), :, pl.ds(at, width)]
            cp = remote(slots, slots, core_s.at[n], core_r.at[n], sib)
            cp.start()
            copies[n, 7] = cp
        for n in range(3 * half, 3 * half + 3):
            copies[n, 7].wait_recv()
        lo = half * 1024

        def grads(j, _):
            cols = pl.ds(pl.multiple_of(lo + j * 256, 256), 256)
            v = dot(hid[...], dz_all[:, :, cols].reshape(2048, 256), ((1,), (0,)))
            msg_w[:, :, cols] = v.astype(BF16).reshape(16, 16, 256)
            return 0

        lax.fori_loop(0, 4, grads, 0)
        for k in range(16):
            hx, hl, hc = (x + k % 4) % 4, (zb + k // 4 % 2) % 2, (c + k // 8) % 2
            cols = pl.ds(lo, 1024)
            piece = msg_w.at[hx + 4 * hl + 8 * hc, :, cols]
            to = (hx, by, 2 * bz + hl, hc)
            into = part_w.at[q, :, cols]
            cp = remote(piece, into, mw_s.at[half, k], mw_r.at[half, q], to)
            if k == 0:
                keep = pltpu.make_async_copy(piece, into, mw_r.at[half, q])
                first.append(cp)

                @pl.when(mine == 0)
                def _():
                    cp.start()

                @pl.when(mine == 1)
                def _():
                    keep.start()

            else:
                cp.start()
                parts.append(cp)
        if half == 0:
            to_far.wait_recv()

        def back(t, _):
            rows = pl.ds(t * 4, 4)
            v = dot(
                dz_all[rows, :, lo : lo + 1024].reshape(512, 1024),
                w_b[:, lo : lo + 1024],
                ((1,), (1,)),
            ).reshape(4, 128, 256)
            if half == 0:
                dh[rows] = v
            else:
                v = v + dh[rows]
                dh[rows] = v
                dh_b[rows] = v.astype(BF16)
            return 0

        lax.fori_loop(0, 4, back, 0)

    grad_cols = band_cols
    dh_full[:, grad_cols] = dh_b[g]
    for k in range(1, 16):
        to = flip(me, k)
        cp = remote(
            dh_b.at[cube_index(to)], dh_full.at[:, grad_cols], dh_s.at[k], dh_r.at[k], to
        )
        cp.start()
        gates.append(cp)

    def products(t, _):
        v2[t] = (dh[t] * nrm[t]).astype(BF16)
        return 0

    lax.fori_loop(0, 16, products, 0)
    sums = dot(o2[:, :2048], dh_b[...].reshape(2048, 256), ((1,), (0,)))
    sums = sums + dot(o2[:, 2048:], v2[...].reshape(2048, 256), ((1,), (0,)))
    for cp in gates[:15]:
        cp.wait_recv()
    gate_sum = gm_b[0].astype(F32)
    for t in range(1, 16):
        gate_sum = gate_sum + gm_b[t].astype(F32)
    at_row = lax.broadcasted_iota(jnp.int32, (256, 64), 0)
    image = lax.broadcasted_iota(jnp.int32, (256, 64), 1)
    put = (at_row % 16 < 4) & (image == at_row // 16 * 4 + at_row % 16)
    spaced = dot(
        jnp.where(put, 1.0, 0.0).astype(BF16), gate_sum.astype(BF16), ((1,), (0,))
    ).astype(BF16)
    for i in range(16):
        rows = slice(8 * i, 8 * i + 8)
        msg_s[i, 0] = jnp.concatenate([sums[rows, :128], sums[rows, 128:]], axis=0).astype(BF16)
        msg_s[i, 1] = spaced[16 * i : 16 * i + 16]
    for k in range(16):
        hx, hl, hc = (x + k % 4) % 4, (zb + k // 4 % 2) % 2, (c + k // 8) % 2
        piece = msg_s.at[hx + 4 * hl + 8 * hc]
        to = (hx, by, 2 * bz + hl, hc)
        cp = remote(piece, part_s.at[q], ms_s.at[k], ms_r.at[q], to)
        if k == 0:
            keep_s = pltpu.make_async_copy(piece, part_s.at[q], ms_r.at[q])
            first.append(cp)

            @pl.when(mine == 0)
            def _():
                cp.start()

            @pl.when(mine == 1)
            def _():
                keep_s.start()

        else:
            cp.start()
            parts.append(cp)

    rest = []
    for half in range(2):
        cols = slice(half * 1024, half * 1024 + 1024)
        for k in range(16):
            into = part_w.at[k, :, cols]
            pltpu.make_async_copy(into, into, mw_r.at[half, k]).wait()
        total = part_w[0, :, cols].astype(F32)
        for k in range(1, 16):
            total = total + part_w[k, :, cols].astype(F32)
        wp[:, cols] = (total * 32768 ** (-0.5)).astype(BF16)
    own_w = pltpu.make_async_copy(wp, o_w.at[h], loc.at[0])
    own_w.start()
    for k, to in enumerate(line):
        cp = remote(wp, o_w.at[h], wp_s.at[k], wp_r.at[k], to)
        cp.start()
        rest.append(cp)

    for k in range(16):
        pltpu.make_async_copy(part_s.at[k], part_s.at[k], ms_r.at[k]).wait()
    total = part_s[0].astype(F32)
    for k in range(1, 16):
        total = total + part_s[k].astype(F32)
    s_own[...] = (total * MEAN_IMG ** (-0.5)).astype(BF16)
    s1[kept] = s_own[...]
    firsts = []
    for k, to in enumerate(plane):
        cp = remote(s_own, s1.at[kept], s1_s.at[k], s1_r.at[k], to)
        cp.start()
        firsts.append(cp)

    for cp in gates[15:]:
        cp.wait_recv()

    def finish(i, _):
        rows = pl.ds(pl.multiple_of(i * 16, 16), 16)
        r, m = rm[rows, 0:1], rm[rows, 1:2]
        normed = (acts_v[rows, :].astype(F32) - m) * r
        dn = dh_full[rows, :].astype(F32) * sc1[rows, :]
        mean = jnp.mean(dn, axis=1, keepdims=True)
        along = jnp.mean(dn * normed, axis=1, keepdims=True)
        o_acts[rows, :] = (r * (dn - mean - normed * along)).astype(BF16)
        return 0

    lax.fori_loop(0, 4, finish, 0)
    for cp in firsts:
        cp.wait_recv()
    s_mod[h] = s1[:, 0]
    gd[h] = jnp.concatenate([s1[k, 1].astype(F32)[:4] for k in range(16)], axis=0).astype(BF16)
    for k, to in enumerate(line):
        for v, ss_, rs_ in ((s_mod, sm_s, sm_r), (gd, gd_s, gd_r)):
            cp = remote(v.at[h], v.at[h], ss_.at[k], rs_.at[k], to)
            cp.start()
            rest.append(cp)
    lax.fori_loop(4, 8, finish, 0)

    own_w.wait()
    for cp in rest[:7]:
        cp.wait_recv()
    mates = pl.ds(c * 8, 8)
    last = [remote(o_w.at[mates], o_w.at[mates], co_s.at[0], co_r.at[0], sib)]
    last[0].start()
    for cp in rest[7:]:
        cp.wait_recv()
    for i, v in ((1, s_mod), (2, gd)):
        cp = remote(v.at[mates], v.at[mates], co_s.at[i], co_r.at[i], sib)
        cp.start()
        last.append(cp)
    last[1].wait_recv()
    last[2].wait_recv()

    def write(i, _):
        images = pl.ds(i * 4, 4)
        for k in range(16):
            v = s_mod[i, k].astype(F32)
            o_mod[images, :, k * 256 : k * 256 + 128] = v[:8].reshape(4, 2, 128)
            o_mod[images, :, k * 256 + 128 : k * 256 + 256] = v[8:].reshape(4, 2, 128)
        return 0

    lax.fori_loop(0, 16, write, 0)
    for i in range(16):
        v = gd[i].astype(F32)
        for k in range(16):
            o_gate[4 * i : 4 * i + 4, k * 128 : k * 128 + 128] = v[4 * k : 4 * k + 4]

    last[0].wait_recv()
    for cp in copies.values():
        cp.wait_send()
    for cp in blocks + gates + parts + firsts + rest + last:
        cp.wait_send()

    @pl.when(mine == 0)
    def _():
        for cp in first:
            cp.wait_send()

    @pl.when(sends_far == 1)
    def _():
        to_far.wait_send()

    @pl.when(swaps == 1)
    def _():
        to_near.wait_send()


def on_device(acts, out_grad, saved_proj, weight, shift_scale, gate, image_of):
    n = len(CHUNKS)
    dma = pltpu.SemaphoreType.DMA
    hbm = pl.BlockSpec(memory_space=pl.ANY)
    local = pl.BlockSpec(memory_space=pltpu.VMEM)
    vmem = pltpu.VMEM
    o_acts, o_w, o_mod, o_gate = pl.pallas_call(
        block_kernel,
        out_shape=(
            jax.ShapeDtypeStruct((128, 4096), BF16),
            jax.ShapeDtypeStruct((16, 16, 2048), BF16),
            jax.ShapeDtypeStruct((64, 2, 4096), F32),
            jax.ShapeDtypeStruct((64, 2048), F32),
        ),
        in_specs=[hbm] * 6 + [local],
        out_specs=(local, hbm, local, local),
        scratch_shapes=[
            vmem((128, 4096), BF16), vmem((128, 2048), BF16), vmem((128, 2048), BF16),
            vmem((64, 2048), F32), vmem((64, 2, 4096), F32), vmem((64, 2, 256), F32),
            vmem((128, 128), F32), vmem((8, 128), F32), vmem((16, 128, 2048), BF16),
            vmem((16, 128, 256), BF16), vmem((16, 8, 128), F32), vmem((64, 2048), BF16),
            vmem((16, 64, 128), BF16), vmem((256, 2048), BF16),
            vmem((256, 2048), BF16), vmem((16, 128, 256), F32), vmem((16, 128, 256), F32),
            vmem((16, 128, 256), BF16), vmem((16, 16, 2048), BF16),
            vmem((16, 2, 16, 128), BF16), vmem((16, 16, 2048), BF16),
            vmem((16, 2, 16, 128), BF16), vmem((128, 4096), BF16), vmem((128, 4096), F32),
            vmem((16, 2048), BF16), vmem((2, 16, 128), BF16), vmem((16, 2, 16, 128), BF16),
            vmem((16, 16, 16, 128), BF16), vmem((16, 64, 128), BF16),
            vmem((128, 4096), BF16), vmem((16, 128, 256), BF16),
            dma((n, 7)), dma((n, 7)), dma((n,)), dma((n,)),
            dma((16,)), dma((16,)), dma((16,)), dma((16,)), dma((16,)), dma((16,)),
            dma((2,)), dma,
            dma((16,)), dma((16,)), dma((2, 16)), dma((2, 16)), dma((16,)), dma((16,)),
            dma((15,)), dma((15,)), dma((7,)), dma((7,)), dma((7,)), dma((7,)),
            dma((7,)), dma((7,)), dma((3,)), dma((3,)), dma((7,)),
        ],
        compiler_params=pltpu.CompilerParams(
            collective_id=0, has_side_effects=True, vmem_limit_bytes=52 * 2**20
        ),
        name="adaln_backward",
    )(acts, out_grad, saved_proj, weight, shift_scale, gate, image_of.reshape(1, 128))
    return o_acts, o_w.reshape(256, 2048), o_mod, o_gate


def solution(mesh):
    placed = (
        P(("rep", "shard"), None),
        P(("rep", "shard"), None),
        P(("rep", "shard"), None),
        P("shard", None),
        P(),
        P(),
        P(("rep", "shard")),
    )
    return jax.shard_map(
        on_device,
        mesh=mesh,
        in_specs=placed,
        out_specs=(P(("rep", "shard"), None), P("shard", None), P(), P()),
        check_vma=False,
    )
```

```python
import jax
import jax.numpy as jnp
from jax import lax
from jax.experimental import pallas as pl
from jax.experimental.pallas import tpu as pltpu
from jax.sharding import PartitionSpec as P

MEAN_IMG = 512
MESH = pl.DeviceIdType.MESH
BF16 = jnp.bfloat16
F32 = jnp.float32
CHUNKS = (
    (0, 128, (0, 1, 2)),
    (128, 384, (1, 2, 0)),
    (512, 512, (2, 0, 1)),
    (1024, 128, (0, 1, 2)),
    (1152, 384, (1, 2, 0)),
    (1536, 512, (2, 0, 1)),
)


def signal(at):
    pl.semaphore_signal(
        pltpu.get_barrier_semaphore(), inc=1, device_id=at, device_id_type=MESH
    )


def remote(src, dst, ss, rs, at):
    return pltpu.make_async_remote_copy(
        src_ref=src,
        dst_ref=dst,
        send_sem=ss,
        recv_sem=rs,
        device_id=at,
        device_id_type=MESH,
    )


class Place:
    def __init__(self):
        r, s = lax.axis_index("rep"), lax.axis_index("shard")
        self.r, self.s = r, s
        self.zb, self.x, self.c = lax.div(r, 8), lax.rem(lax.div(r, 2), 4), lax.rem(r, 2)
        self.y, self.zh = lax.div(s, 4), lax.rem(s, 4)
        self.xb, self.yb = lax.rem(self.x, 2), lax.rem(self.y, 2)
        self.xh, self.yh = lax.div(self.x, 2), lax.div(self.y, 2)
        self.odd = lax.rem(self.zh, 2)
        bits = (self.xb, self.yb, self.zb, self.c)
        self.turn = [1 - 2 * b for b in bits]
        self.slot0 = self.xb + 2 * self.yb + 4 * self.zb + 8 * self.c
        p = lax.rem(self.xb + self.c, 2)
        e = lax.rem(self.zb + self.odd, 2)
        self.p, self.e = p, e
        self.e0 = 1 - e
        ys = (self.y, self.y + self.turn[1])
        self.band_y = [[v + w * (3 - 2 * v) for w in (p, 1 - p)] for v in ys]
        self.band_z = []
        for kz in range(2):
            zb, ev = (1 - self.zb, 1 - e) if kz else (self.zb, e)
            row = []
            for kc in range(2):
                c = 1 - self.c if kc else self.c
                row.append(lax.rem(self.zh + c * (2 * zb + 3) + (1 - c) * 2 * (1 - ev), 4))
            self.band_z.append(row)
        self.xs = [lax.rem(self.x + k, 4) for k in range(4)]
        self.ys = [lax.rem(self.y + k, 4) * 4 for k in range(4)]
        self.zs = [lax.rem(self.zh + k, 4) for k in range(4)]

    def mate(self, k):
        r = self.r
        for bit, step in ((0, 2), (2, 8), (3, 1)):
            if k >> bit & 1:
                r = r + step * self.turn[bit]
        return r, self.s + 4 * self.turn[1] if k & 2 else self.s

    def slot(self, k):
        v = self.slot0
        for bit in range(4):
            if k >> bit & 1:
                v = v + (1 << bit) * self.turn[bit]
        return v

    def band(self, k):
        kx, ky, kz, kc = (k >> i & 1 for i in range(4))
        return 4 * self.band_y[ky][kx ^ kc] + self.band_z[kz][kc]

    def far(self):
        z = 2 * self.zh + self.zb + (2 * self.zb - 1) * (3 - 2 * self.c) + 8
        y = self.y + self.p * (3 - 2 * self.y)
        return lax.rem(z, 2) * 8 + self.x * 2 + self.c, y * 4 + lax.rem(lax.div(z, 2), 4)

    def pair(self):
        return self.zb * 8 + (3 - self.x) * 2 + self.c, (3 - self.y) * 4 + self.zh

    def near(self):
        return self.r, (3 - self.y) * 4 + self.zh

    def senders(self):
        found = []
        for k in range(16):
            kx, ky, kz = k % 2, k // 2 % 2, k // 4
            d = (4 - kz) % 4
            c = d % 2
            if c:
                zb = (3 - d) // 2
            else:
                zb = 1 - self.odd if (1 + d // 2 + kz) % 2 else self.odd
            xh = 1 - self.xh if kx else self.xh
            y = 3 - self.y if ky else self.y
            found.append((zb * 8 + (2 * xh + (ky + c) % 2) * 2 + c, y * 4 + self.zs[kz]))
        return found

    def holders(self, band):
        zs, cs = (self.zb, 1 - self.zb), (self.c, 1 - self.c)
        return [
            (
                2 * self.xs[k % 4] + zs[k // 4 % 2] + 8 * cs[k // 8],
                (zs[k // 4 % 2] * 8 + self.xs[k % 4] * 2 + cs[k // 8], band),
            )
            for k in range(16)
        ]

    def near_holders(self, band):
        far = 1 - (1 - self.c) * self.e
        zb = self.zb + self.turn[2] * far
        cs = (self.c, 1 - self.c)
        return [
            (
                2 * self.xs[k % 4] + 8 * cs[k // 4],
                (zb * 8 + self.xs[k % 4] * 2 + cs[k // 4], band),
            )
            for k in range(8)
        ]

    def plane(self):
        return [(self.r, self.ys[k // 4] + self.zs[k % 4]) for k in range(1, 16)]

    def line(self):
        zs = (self.zb, 1 - self.zb)
        return [(zs[k // 4] * 8 + self.xs[k % 4] * 2 + self.c, self.s) for k in range(1, 8)]


def dot(a, b, dims):
    return lax.dot_general(a, b, (dims, ((), ())), preferred_element_type=F32)


def two_terms(v):
    hi = v.astype(BF16)
    return hi, (v - hi.astype(F32)).astype(BF16)


def image_hot(ids, count):
    rows = lax.broadcasted_iota(jnp.int32, (count, ids.shape[1]), 0).astype(F32)
    return jnp.where(rows == ids, 1.0, 0.0)


def block_kernel(
    acts, og, sp, w, ss, gate, ids,
    o_acts, o_w, o_mod, o_gate,
    acts_v, og_v, sp_v, gate_v, ss_v, ss_b, rm, st, dz_all, acts_b, st_b,
    gm, gm_o, gm_i, gm_t, gm_b, w_b, hid, nrm, dh, dh_b, msg_a, msg_b, msg_s, part_a, part_b, part_s,
    dh_full, sc1, wp, s_own, s1, rec, o2, v2, acc, to_z, from_z, at_z,
    dz_s, dz_r, core_s, core_r, ac_s, ac_r, st_s, st_r, gm_s, gm_r, w_s, w_r,
    dh_s, dh_r, mw_s, mw_r, ms_s, ms_r, s1_s, s1_r, wp_s, wp_r, sm_s, sm_r, co_s, co_r, tz_s, tz_r, loc,
):
    me = Place()
    c, g, b = me.c, me.slot0, me.band(0)
    far, near = me.far(), me.near()
    keeps = (1 - c) * me.e * (1 - me.p)
    swaps = (1 - c) * me.e * me.p
    takes_half = (1 - c) * (1 - me.e)
    pair = me.pair()
    mine = keeps
    q = me.xh + 2 * me.yh + 4 * me.zh
    h = 2 * me.x + me.zb + 8 * c
    kept = me.s
    sib = me.mate(8)
    plane, line = me.plane(), me.line()
    cz = 2 * c + me.zb
    octet = g - 8 * c
    band_cols = pl.ds(pl.multiple_of(b * 256, 256), 256)

    def own_core(bits, at, width):
        return dz_all.at[
            pl.ds(2 * c, 2) if bits & 4 else cz,
            pl.ds(0, 2) if bits & 2 else me.yb,
            pl.ds(0, 2) if bits & 1 else me.xb,
            :,
            pl.ds(at, width),
        ]

    loads = [
        pltpu.make_async_copy(a, v, loc.at[i])
        for i, (a, v) in enumerate(
            ((og, og_v), (gate, gate_v), (acts, acts_v), (sp, sp_v),
             (ss.at[:, :, band_cols], ss_b), (ss, ss_v), (acts.at[:, band_cols], acts_b.at[g]))
        )
    ]
    for cp in loads:
        cp.start()
    for k in range(1, 16):
        signal(me.mate(k))
    signal(far)

    @pl.when(swaps == 1)
    def _():
        signal(near)

    @pl.when(takes_half == 1)
    def _():
        signal(pair)

    senders = me.senders()

    @pl.when(mine == 0)
    def _():
        signal(senders[0])

    for to in senders[1:]:
        signal(to)
    for to in plane + line:
        signal(to)

    ids_f = ids[...].astype(F32)
    hot = image_hot(ids_f, 128)
    hot_t = hot.T[:, :64].astype(BF16)
    loads[0].wait()
    loads[1].wait()
    for j in range(0, 2048, 512):
        cols = slice(j, j + 512)
        hi, lo = two_terms(gate_v[:, cols])
        rows = dot(hot_t, hi, ((1,), (0,))) + dot(hot_t, lo, ((1,), (0,)))
        dz_all[cz, me.yb, me.xb, :, cols] = (rows * og_v[:, cols].astype(F32)).astype(BF16)

    pl.semaphore_wait(pltpu.get_barrier_semaphore(), 54 + swaps + takes_half - mine)

    copies = {}

    def stage(k, half):
        for n in range(3 * half, 3 * half + 3):
            at, width, order = CHUNKS[n]
            if k:
                copies[n, k - 1].wait_recv()
            slots = own_core(sum(1 << d for d in order[:k]), at, width)
            cp = remote(slots, slots, dz_s.at[n, k], dz_r.at[n, k], me.mate(1 << order[k]))
            cp.start()
            copies[n, k] = cp

    stage(0, 0)

    half_rows = pl.ds(pl.multiple_of(128 * lax.div(me.x, 2), 128), 128)
    to_far = remote(w, w_b, w_s.at[0], w_r.at[0], far)
    to_near = remote(w, w_b, w_s.at[1], w_r.at[0], near)
    to_self = pltpu.make_async_copy(w, w_b, w_r.at[0])
    half_far = remote(w.at[half_rows], w_b.at[half_rows], w_s.at[2], w_r.at[1], far)
    half_twin = remote(w_b.at[half_rows], w_b.at[half_rows], w_s.at[3], w_r.at[2], pair)

    @pl.when(c == 1)
    def _():
        to_far.start()

    @pl.when((1 - c) * me.e == 1)
    def _():
        half_far.start()

    @pl.when(swaps == 1)
    def _():
        to_near.start()

    @pl.when(keeps == 1)
    def _():
        to_self.start()

    loads[2].wait()

    def stats(i, _):
        rows = pl.ds(pl.multiple_of(i * 16, 16), 16)
        v = acts_v[rows, :].astype(F32)
        m = jnp.mean(v, axis=1, keepdims=True)
        v = v - m
        r = lax.rsqrt(jnp.mean(v * v, axis=1, keepdims=True) + 1e-06)
        lane = lax.broadcasted_iota(jnp.int32, (16, 128), 1)
        rm[rows, :] = jnp.where(lane == 0, r, jnp.where(lane == 1, m, 0.0))
        return 0

    lax.fori_loop(0, 8, stats, 0)
    turned = rm[...].T[:8, :]
    row = lax.broadcasted_iota(jnp.int32, (8, 128), 0)
    st[...] = jnp.where(row == 2, ids_f, turned)
    st_b[g] = st[...]

    stage(1, 0)
    stage(0, 1)

    blocks = []
    for k in range(1, 16):
        cols = pl.ds(pl.multiple_of(me.band(k) * 256, 256), 256)
        cp = remote(acts.at[:, cols], acts_b.at[g], ac_s.at[k], ac_r.at[k], me.mate(k))
        cp.start()
        blocks.append(cp)

    for k in range(1, 16):
        cp = remote(st, st_b.at[g], st_s.at[k], st_r.at[k], me.mate(k))
        cp.start()
        blocks.append(cp)

    loads[3].wait()
    hot_b = hot[:64].astype(BF16)
    for j in range(0, 2048, 512):
        cols = slice(j, j + 512)
        hi, lo = two_terms(og_v[:, cols].astype(F32) * sp_v[:, cols].astype(F32))
        gm[:, cols] = (dot(hot_b, hi, ((1,), (0,))) + dot(hot_b, lo, ((1,), (0,)))).astype(BF16)
    for k in range(16):
        gm_o[me.slot(k)] = gm[:, pl.ds(pl.multiple_of(me.band(k) * 128, 128), 128)]
    swap = remote(gm_o.at[pl.ds(8 - 8 * c, 8)], gm_i, gm_s.at[0], gm_r.at[0], sib)
    swap.start()

    stage(2, 0)
    stage(1, 1)

    @pl.when(takes_half == 1)
    def _():
        half_far.wait_recv()
        half_twin.start()

    stage(2, 1)

    loads[5].wait()

    def scales(j, _):
        cols = pl.ds(pl.multiple_of(j * 512, 512), 512)
        hi, lo = two_terms(ss_v[:, 1, cols])
        sc1[:, cols] = 1.0 + (dot(hot_t, hi, ((1,), (0,))) + dot(hot_t, lo, ((1,), (0,))))
        return 0

    lax.fori_loop(0, 8, scales, 0)

    loads[4].wait()
    loads[6].wait()
    for cp in blocks:
        cp.wait_recv()
    shift_hi, shift_lo = two_terms(ss_b[:, 0, :])
    scale_hi, scale_lo = two_terms(ss_b[:, 1, :])
    tables = jnp.concatenate(
        [
            jnp.concatenate([shift_hi, scale_hi], axis=1),
            jnp.concatenate([shift_lo, scale_lo], axis=1),
        ],
        axis=0,
    )

    def modulate(t, _):
        block = st_b[t]
        wide = jnp.concatenate([block, jnp.zeros((120, 128), F32)], axis=0).T
        r, m = wide[:, 0:1], wide[:, 1:2]
        own = image_hot(block[2:3], 64)
        twice = jnp.concatenate([own, own], axis=0).T.astype(BF16)
        mods = dot(twice, tables, ((1,), (0,)))
        normed = (acts_b[t].astype(F32) - m) * r
        nrm[t] = normed
        out = normed * (1.0 + mods[:, 256:]) + mods[:, :256]
        hid[:, pl.ds(pl.multiple_of(t * 128, 128), 128)] = out.T.astype(BF16)
        rows = lax.broadcasted_iota(jnp.int32, (128, 128), 0)
        hit = ((rows // 2).astype(F32) == block[2:3])
        o2[:, pl.ds(pl.multiple_of(t * 128, 128), 128)] = jnp.where(
            hit & (rows % 2 == 0), 1.0, 0.0
        ).astype(BF16)
        o2[:, pl.ds(pl.multiple_of(2048 + t * 128, 128), 128)] = jnp.where(
            hit & (rows % 2 == 1), 1.0, 0.0
        ).astype(BF16)
        return 0

    lax.fori_loop(0, 16, modulate, 0)

    swap.wait_recv()
    gm_t[...] = (gm_o[pl.ds(8 * c, 8)].astype(F32) + gm_i[...].astype(F32)).astype(BF16)
    gm_b[octet] = gm_t[octet]
    gates = []
    for k in range(1, 8):
        cp = remote(
            gm_t.at[me.slot(k) - 8 * c], gm_b.at[octet], gm_s.at[k], gm_r.at[k], me.mate(k)
        )
        cp.start()
        gates.append(cp)

    parts, first = [], []

    def arrive(half):
        for n in range(3 * half, 3 * half + 3):
            at, width, _ = CHUNKS[n]
            copies[n, 2].wait_recv()
            slots = own_core(7, at, width)
            cp = remote(slots, slots, core_s.at[n], core_r.at[n], sib)
            cp.start()
            copies[n, 3] = cp

    def complete(half):
        for n in range(3 * half, 3 * half + 3):
            copies[n, 3].wait_recv()

    def give(pieces, into, ss_, rs_):
        for k, (piece, to) in enumerate(pieces):
            cp = remote(piece, into, ss_.at[k], rs_.at[q], to)
            if k == 0:
                keep = pltpu.make_async_copy(piece, into, rs_.at[q])
                first.append(cp)

                @pl.when(mine == 0)
                def _():
                    cp.start()

                @pl.when(mine == 1)
                def _():
                    keep.start()

            else:
                cp.start()
                parts.append(cp)

    def give_rows(msg, part, half):
        pieces = [(msg.at[pl.ds(i, 2)], to) for i, to in me.near_holders(b)]
        give(pieces, part.at[q], mw_s.at[half], mw_r.at[half])

    def weight_grad(msg, half):
        def grads(j, _):
            cols = pl.ds(pl.multiple_of(half * 1024 + j * 256, 256), 256)
            v = dot(hid[...], dz_all[:, :, :, :, cols].reshape(2048, 256), ((1,), (0,)))
            cols = pl.ds(pl.multiple_of(j * 256, 256), 256)
            msg[:, :, cols] = v.astype(BF16).reshape(16, 16, 256)
            return 0

        lax.fori_loop(0, 4, grads, 0)

    def back(half):
        def some(t, _):
            rows = pl.ds(t * 4, 4)
            v = dot(
                dz_all[t, :, :, :, half * 1024 : half * 1024 + 1024].reshape(512, 1024),
                w_b[:, half * 1024 : half * 1024 + 1024],
                ((1,), (1,)),
            ).reshape(4, 128, 256)
            if half == 0:
                dh[rows] = v
            else:
                v = v + dh[rows]
                dh_b[rows] = v.astype(BF16)
                v2[rows] = (v * nrm[rows]).astype(BF16)
            return 0

        lax.fori_loop(0, 4, some, 0)

    arrive(0)
    complete(0)
    weight_grad(msg_a, 0)
    give_rows(msg_a, part_a, 0)
    arrive(1)

    @pl.when(takes_half == 1)
    def _():
        half_twin.wait_recv()

    @pl.when(takes_half == 0)
    def _():
        to_far.wait_recv()

    back(0)
    for cp in gates[:7]:
        cp.wait_recv()
    gate_sum = gm_b[0].astype(F32)
    for t in range(1, 8):
        gate_sum = gate_sum + gm_b[t].astype(F32)
    at_row = lax.broadcasted_iota(jnp.int32, (256, 64), 0)
    image = lax.broadcasted_iota(jnp.int32, (256, 64), 1)
    put = (at_row % 16 < 4) & (image == at_row // 16 * 4 + at_row % 16)
    spaced = dot(
        jnp.where(put, 1.0, 0.0).astype(BF16), gate_sum.astype(BF16), ((1,), (0,))
    ).astype(BF16)
    msg_s[:, 1] = spaced.reshape(16, 16, 128)
    complete(1)
    back(1)

    sums = dot(o2[:, :2048], dh_b[...].reshape(2048, 256), ((1,), (0,)))
    sums = sums + dot(o2[:, 2048:], v2[...].reshape(2048, 256), ((1,), (0,)))
    for i in range(16):
        rows = slice(8 * i, 8 * i + 8)
        both = jnp.concatenate([sums[rows, :128], sums[rows, 128:]], axis=0)
        msg_s[i, 0] = both.astype(BF16)


    give([(msg_s.at[i], to) for i, to in me.holders(b)], part_s.at[q], ms_s, ms_r)
    dh_full[:, band_cols] = dh_b[g]
    for k in range(1, 16):
        cp = remote(
            dh_b.at[me.slot(k)], dh_full.at[:, band_cols], dh_s.at[k], dh_r.at[k], me.mate(k)
        )
        cp.start()
        gates.append(cp)
    weight_grad(msg_b, 1)
    give_rows(msg_b, part_b, 1)

    comes = (1 - me.e0, me.zb, 1 - me.e0, 1 - me.zb)

    def collect(part, half):
        acc[...] = jnp.zeros_like(acc)
        for kz in range(4):

            @pl.when(comes[kz] == 1)
            def _():
                for k in range(4):
                    at = 4 * me.zs[kz] + k
                    pltpu.make_async_copy(part.at[at], part.at[at], mw_r.at[half, at]).wait()
                total = part[4 * me.zs[kz]].astype(F32)
                for k in range(1, 4):
                    total = total + part[4 * me.zs[kz] + k].astype(F32)
                acc[...] += total

        to_z[half] = acc[1 - me.zb].astype(BF16)
        at_z[half] = acc[me.zb]
        cp = remote(to_z.at[half], from_z.at[half], tz_s.at[half], tz_r.at[half], me.mate(4))
        cp.start()
        return cp

    for k in range(16):
        pltpu.make_async_copy(part_s.at[k], part_s.at[k], ms_r.at[k]).wait()
    total = part_s[0].astype(F32)
    for k in range(1, 16):
        total = total + part_s[k].astype(F32)
    s_own[...] = (total * MEAN_IMG ** (-0.5)).astype(BF16)
    s1[kept] = s_own[...]
    firsts = []
    for k, to in enumerate(plane):
        cp = remote(s_own, s1.at[kept], s1_s.at[k], s1_r.at[k], to)
        cp.start()
        firsts.append(cp)

    def finish(i, _):
        rows = pl.ds(pl.multiple_of(i * 16, 16), 16)
        r, m = rm[rows, 0:1], rm[rows, 1:2]
        normed = (acts_v[rows, :].astype(F32) - m) * r
        dn = dh_full[rows, :].astype(F32) * sc1[rows, :]
        mean = jnp.mean(dn, axis=1, keepdims=True)
        along = jnp.mean(dn * normed, axis=1, keepdims=True)
        o_acts[rows, :] = (r * (dn - mean - normed * along)).astype(BF16)
        return 0

    zed = [collect(part_a, 0)]
    rest = []
    for cp in firsts:
        cp.wait_recv()
    rec[h, :16] = s1[:, 0]
    rec[h, 16:] = (
        jnp.concatenate([s1[k, 1].astype(F32)[:4] for k in range(16)], axis=0)
        .astype(BF16)
        .reshape(4, 16, 128)
    )
    for k, to in enumerate(line):
        cp = remote(rec.at[h], rec.at[h], sm_s.at[k], sm_r.at[k], to)
        cp.start()
        rest.append(cp)
    zed.append(collect(part_b, 1))
    for half in range(2):
        zed[half].wait_recv()
        total = at_z[half] + from_z[half].astype(F32)
        cols = slice(half * 1024, half * 1024 + 1024)
        wp[:, cols] = (total * 32768 ** (-0.5)).astype(BF16)
    own_w = pltpu.make_async_copy(wp, o_w.at[h], loc.at[0])
    own_w.start()
    for k, to in enumerate(line):
        cp = remote(wp, o_w.at[h], wp_s.at[k], wp_r.at[k], to)
        cp.start()
        rest.append(cp)

    for cp in gates[7:]:
        cp.wait_recv()

    lax.fori_loop(0, 8, finish, 0)

    own_w.wait()
    mates = pl.ds(c * 8, 8)
    last = []
    for i, v in ((0, rec), (1, o_w)):
        for cp in rest[7 * i : 7 * i + 7]:
            cp.wait_recv()
        cp = remote(v.at[mates], v.at[mates], co_s.at[i], co_r.at[i], sib)
        cp.start()
        last.append(cp)
    last[0].wait_recv()

    def write(i, _):
        images = pl.ds(i * 4, 4)
        for k in range(16):
            v = rec[i, k].astype(F32)
            o_mod[images, :, k * 256 : k * 256 + 128] = v[:8].reshape(4, 2, 128)
            o_mod[images, :, k * 256 + 128 : k * 256 + 256] = v[8:].reshape(4, 2, 128)
        return 0

    lax.fori_loop(0, 16, write, 0)
    for i in range(16):
        v = rec[i, 16:].reshape(64, 128).astype(F32)
        for k in range(16):
            o_gate[4 * i : 4 * i + 4, k * 128 : k * 128 + 128] = v[4 * k : 4 * k + 4]

    last[1].wait_recv()
    for cp in copies.values():
        cp.wait_send()
    for cp in blocks + [swap] + gates + parts + firsts + rest + last + zed:
        cp.wait_send()

    @pl.when(mine == 0)
    def _():
        for cp in first:
            cp.wait_send()

    @pl.when(c == 1)
    def _():
        to_far.wait_send()

    @pl.when((1 - c) * me.e == 1)
    def _():
        half_far.wait_send()

    @pl.when(takes_half == 1)
    def _():
        half_twin.wait_send()

    @pl.when(swaps == 1)
    def _():
        to_near.wait_send()


def on_device(acts, out_grad, saved_proj, weight, shift_scale, gate, image_of):
    n = len(CHUNKS)
    dma = pltpu.SemaphoreType.DMA
    hbm = pl.BlockSpec(memory_space=pl.ANY)
    local = pl.BlockSpec(memory_space=pltpu.VMEM)
    vmem = pltpu.VMEM
    o_acts, o_w, o_mod, o_gate = pl.pallas_call(
        block_kernel,
        out_shape=(
            jax.ShapeDtypeStruct((128, 4096), BF16),
            jax.ShapeDtypeStruct((16, 16, 2048), BF16),
            jax.ShapeDtypeStruct((64, 2, 4096), F32),
            jax.ShapeDtypeStruct((64, 2048), F32),
        ),
        in_specs=[pl.BlockSpec(memory_space=pltpu.HBM)] * 6 + [local],
        out_specs=(local, hbm, local, local),
        scratch_shapes=[
            vmem((128, 4096), BF16), vmem((128, 2048), BF16), vmem((128, 2048), BF16),
            vmem((64, 2048), F32), vmem((64, 2, 4096), F32), vmem((64, 2, 256), F32),
            vmem((128, 128), F32), vmem((8, 128), F32), vmem((4, 2, 2, 128, 2048), BF16),
            vmem((16, 128, 256), BF16), vmem((16, 8, 128), F32),
            vmem((64, 2048), BF16), vmem((16, 64, 128), BF16), vmem((8, 64, 128), BF16),
            vmem((8, 64, 128), BF16), vmem((8, 64, 128), BF16), vmem((256, 2048), BF16),
            vmem((256, 2048), BF16), vmem((16, 128, 256), F32), vmem((16, 128, 256), F32),
            vmem((16, 128, 256), BF16), vmem((16, 16, 1024), BF16), vmem((16, 16, 1024), BF16),
            vmem((16, 2, 16, 128), BF16), vmem((16, 2, 16, 1024), BF16),
            vmem((16, 2, 16, 1024), BF16), vmem((16, 2, 16, 128), BF16),
            vmem((128, 4096), BF16), vmem((128, 4096), F32), vmem((16, 2048), BF16),
            vmem((2, 16, 128), BF16), vmem((16, 2, 16, 128), BF16),
            vmem((16, 20, 16, 128), BF16), vmem((128, 4096), BF16), vmem((16, 128, 256), BF16),
            vmem((2, 16, 1024), F32), vmem((2, 16, 1024), BF16), vmem((2, 16, 1024), BF16),
            vmem((2, 16, 1024), F32),
            dma((n, 3)), dma((n, 3)), dma((n,)), dma((n,)),
            dma((16,)), dma((16,)), dma((16,)), dma((16,)), dma((8,)), dma((8,)),
            dma((4,)), dma((3,)), dma((16,)), dma((16,)), dma((2, 8)), dma((2, 16)),
            dma((16,)), dma((16,)), dma((15,)), dma((15,)), dma((7,)), dma((7,)), dma((7,)), dma((7,)),
            dma((2,)), dma((2,)), dma((2,)), dma((2,)), dma((7,)),
        ],
        compiler_params=pltpu.CompilerParams(
            collective_id=0, has_side_effects=True, vmem_limit_bytes=60 * 2**20
        ),
        name="adaln_backward",
    )(acts, out_grad, saved_proj, weight, shift_scale, gate, image_of.reshape(1, 128))
    return o_acts, o_w.reshape(256, 2048), o_mod, o_gate


def solution(mesh):
    placed = (
        P(("rep", "shard"), None),
        P(("rep", "shard"), None),
        P(("rep", "shard"), None),
        P("shard", None),
        P(),
        P(),
        P(("rep", "shard")),
    )
    return jax.shard_map(
        on_device,
        mesh=mesh,
        in_specs=placed,
        out_specs=(P(("rep", "shard"), None), P("shard", None), P(), P()),
        check_vma=False,
    )
```

```python
import jax
import jax.numpy as jnp
from jax import lax
from jax.experimental import pallas as pl
from jax.experimental.pallas import tpu as pltpu
from jax.sharding import PartitionSpec as P

MEAN_IMG = 512
MESH = pl.DeviceIdType.MESH
BF16 = jnp.bfloat16
F32 = jnp.float32
CHUNKS = (
    (0, 128, (0, 1, 2)),
    (128, 256, (1, 2, 0)),
    (384, 384, (2, 0, 1)),
    (768, 256, (0, 1, 2)),
    (1024, 512, (1, 2, 0)),
    (1536, 512, (2, 0, 1)),
)
SPLIT = 768
WIDE = (768, 1280)


def signal(at):
    pl.semaphore_signal(
        pltpu.get_barrier_semaphore(), inc=1, device_id=at, device_id_type=MESH
    )


def remote(src, dst, ss, rs, at):
    return pltpu.make_async_remote_copy(
        src_ref=src,
        dst_ref=dst,
        send_sem=ss,
        recv_sem=rs,
        device_id=at,
        device_id_type=MESH,
    )


class Place:
    def __init__(self):
        r, s = lax.axis_index("rep"), lax.axis_index("shard")
        self.r, self.s = r, s
        self.zb, self.x, self.c = lax.div(r, 8), lax.rem(lax.div(r, 2), 4), lax.rem(r, 2)
        self.y, self.zh = lax.div(s, 4), lax.rem(s, 4)
        self.xb, self.yb = lax.rem(self.x, 2), lax.rem(self.y, 2)
        self.xh, self.yh = lax.div(self.x, 2), lax.div(self.y, 2)
        self.odd = lax.rem(self.zh, 2)
        bits = (self.xb, self.yb, self.zb, self.c)
        self.turn = [1 - 2 * b for b in bits]
        self.slot0 = self.xb + 2 * self.yb + 4 * self.zb + 8 * self.c
        p = lax.rem(self.xb + self.c, 2)
        e = lax.rem(self.zb + self.odd, 2)
        self.p, self.e = p, e
        self.e0 = 1 - e
        ys = (self.y, self.y + self.turn[1])
        self.band_y = [[v + w * (3 - 2 * v) for w in (p, 1 - p)] for v in ys]
        self.band_z = []
        for kz in range(2):
            zb, ev = (1 - self.zb, 1 - e) if kz else (self.zb, e)
            row = []
            for kc in range(2):
                c = 1 - self.c if kc else self.c
                row.append(lax.rem(self.zh + c * (2 * zb + 3) + (1 - c) * 2 * (1 - ev), 4))
            self.band_z.append(row)
        self.xs = [lax.rem(self.x + k, 4) for k in range(4)]
        self.ys = [lax.rem(self.y + k, 4) * 4 for k in range(4)]
        self.zs = [lax.rem(self.zh + k, 4) for k in range(4)]

    def mate(self, k):
        r = self.r
        for bit, step in ((0, 2), (2, 8), (3, 1)):
            if k >> bit & 1:
                r = r + step * self.turn[bit]
        return r, self.s + 4 * self.turn[1] if k & 2 else self.s

    def slot(self, k):
        v = self.slot0
        for bit in range(4):
            if k >> bit & 1:
                v = v + (1 << bit) * self.turn[bit]
        return v

    def band(self, k):
        kx, ky, kz, kc = (k >> i & 1 for i in range(4))
        return 4 * self.band_y[ky][kx ^ kc] + self.band_z[kz][kc]

    def far(self):
        z = 2 * self.zh + self.zb + (2 * self.zb - 1) * (3 - 2 * self.c) + 8
        y = self.y + self.p * (3 - 2 * self.y)
        return lax.rem(z, 2) * 8 + self.x * 2 + self.c, y * 4 + lax.rem(lax.div(z, 2), 4)

    def pair(self):
        return self.zb * 8 + (3 - self.x) * 2 + self.c, (3 - self.y) * 4 + self.zh

    def near(self):
        return self.r, (3 - self.y) * 4 + self.zh

    def senders(self):
        found = []
        for k in range(16):
            kx, ky, kz = k % 2, k // 2 % 2, k // 4
            d = (4 - kz) % 4
            c = d % 2
            if c:
                zb = (3 - d) // 2
            else:
                zb = 1 - self.odd if (1 + d // 2 + kz) % 2 else self.odd
            xh = 1 - self.xh if kx else self.xh
            y = 3 - self.y if ky else self.y
            found.append((zb * 8 + (2 * xh + (ky + c) % 2) * 2 + c, y * 4 + self.zs[kz]))
        return found

    def holders(self, band):
        zs, cs = (self.zb, 1 - self.zb), (self.c, 1 - self.c)
        return [
            (
                2 * self.xs[k % 4] + zs[k // 4 % 2] + 8 * cs[k // 8],
                (zs[k // 4 % 2] * 8 + self.xs[k % 4] * 2 + cs[k // 8], band),
            )
            for k in range(16)
        ]

    def near_holders(self, band):
        far = 1 - (1 - self.c) * self.e
        zb = self.zb + self.turn[2] * far
        cs = (self.c, 1 - self.c)
        return [
            (
                2 * self.xs[k % 4] + 8 * cs[k // 4],
                (zb * 8 + self.xs[k % 4] * 2 + cs[k // 4], band),
            )
            for k in range(8)
        ]

    def plane(self):
        return [(self.r, self.ys[k // 4] + self.zs[k % 4]) for k in range(1, 16)]

    def line(self):
        zs = (self.zb, 1 - self.zb)
        return [(zs[k // 4] * 8 + self.xs[k % 4] * 2 + self.c, self.s) for k in range(1, 8)]


def dot(a, b, dims):
    return lax.dot_general(a, b, (dims, ((), ())), preferred_element_type=F32)


def two_terms(v):
    hi = v.astype(BF16)
    return hi, (v - hi.astype(F32)).astype(BF16)


def image_hot(ids, count):
    rows = lax.broadcasted_iota(jnp.int32, (count, ids.shape[1]), 0).astype(F32)
    return jnp.where(rows == ids, 1.0, 0.0)


def block_kernel(
    acts, og, sp, w, ss, gate, ids,
    o_acts, o_w, o_rec,
    acts_v, og_v, sp_v, gate_v, ss_v, ss_b, rm, st, dz_all, acts_b, st_b,
    gm, gm_o, gm_i, gm_t, gm_b, w_b, hid, nrm, dh, dh_b, msg_a, msg_b, msg_s, part_a, part_b, part_s,
    dh_full, sc1, wp, s_own, s1, rec, ga, o2, v2, acc, to_z, from_z, at_z,
    dz_s, dz_r, core_s, core_r, ac_s, ac_r, st_s, st_r, gm_s, gm_r, w_s, w_r,
    dh_s, dh_r, mw_s, mw_r, ms_s, ms_r, s1_s, s1_r, wp_s, wp_r, sm_s, sm_r, co_s, co_r, tz_s, tz_r, loc,
):
    me = Place()
    c, g, b = me.c, me.slot0, me.band(0)
    far, near = me.far(), me.near()
    keeps = (1 - c) * me.e * (1 - me.p)
    swaps = (1 - c) * me.e * me.p
    takes_half = (1 - c) * (1 - me.e)
    pair = me.pair()
    mine = keeps
    q = me.xh + 2 * me.yh + 4 * me.zh
    h = 2 * me.x + me.zb + 8 * c
    kept = me.s
    sib = me.mate(8)
    plane, line = me.plane(), me.line()
    cz = 2 * c + me.zb
    octet = g - 8 * c
    band_cols = pl.ds(pl.multiple_of(b * 256, 256), 256)

    def own_core(bits, at, width):
        return dz_all.at[
            pl.ds(2 * c, 2) if bits & 4 else cz,
            pl.ds(0, 2) if bits & 2 else me.yb,
            pl.ds(0, 2) if bits & 1 else me.xb,
            :,
            pl.ds(at, width),
        ]

    loads = [
        pltpu.make_async_copy(a, v, loc.at[i])
        for i, (a, v) in enumerate(
            ((og, og_v), (gate, gate_v), (acts, acts_v), (sp, sp_v),
             (ss.at[:, :, band_cols], ss_b), (ss, ss_v), (acts.at[:, band_cols], acts_b.at[g]))
        )
    ]
    for cp in loads:
        cp.start()
    for k in range(1, 16):
        signal(me.mate(k))
    signal(far)

    @pl.when(swaps == 1)
    def _():
        signal(near)

    @pl.when(takes_half == 1)
    def _():
        signal(pair)

    senders = me.senders()

    @pl.when(mine == 0)
    def _():
        signal(senders[0])

    for to in senders[1:]:
        signal(to)
    for to in plane + line:
        signal(to)

    ids_f = ids[...].astype(F32)
    hot = image_hot(ids_f, 128)
    hot_t = hot.T[:, :64].astype(BF16)
    loads[0].wait()
    loads[1].wait()
    for j in range(0, 2048, 512):
        cols = slice(j, j + 512)
        hi, lo = two_terms(gate_v[:, cols])
        rows = dot(hot_t, hi, ((1,), (0,))) + dot(hot_t, lo, ((1,), (0,)))
        dz_all[cz, me.yb, me.xb, :, cols] = (rows * og_v[:, cols].astype(F32)).astype(BF16)

    pl.semaphore_wait(pltpu.get_barrier_semaphore(), 54 + swaps + takes_half - mine)

    copies = {}

    def stage(k, half):
        for n in range(3 * half, 3 * half + 3):
            at, width, order = CHUNKS[n]
            if k:
                copies[n, k - 1].wait_recv()
            slots = own_core(sum(1 << d for d in order[:k]), at, width)
            cp = remote(slots, slots, dz_s.at[n, k], dz_r.at[n, k], me.mate(1 << order[k]))
            cp.start()
            copies[n, k] = cp

    stage(0, 0)

    half_rows = pl.ds(pl.multiple_of(128 * lax.div(me.x, 2), 128), 128)
    to_far = remote(w, w_b, w_s.at[0], w_r.at[0], far)
    to_near = remote(w, w_b, w_s.at[1], w_r.at[0], near)
    to_self = pltpu.make_async_copy(w, w_b, w_r.at[0])
    half_far = remote(w.at[half_rows], w_b.at[half_rows], w_s.at[2], w_r.at[1], far)
    half_twin = remote(w_b.at[half_rows], w_b.at[half_rows], w_s.at[3], w_r.at[2], pair)

    @pl.when(c == 1)
    def _():
        to_far.start()

    @pl.when((1 - c) * me.e == 1)
    def _():
        half_far.start()

    @pl.when(swaps == 1)
    def _():
        to_near.start()

    @pl.when(keeps == 1)
    def _():
        to_self.start()

    loads[2].wait()

    def stats(i, _):
        rows = pl.ds(pl.multiple_of(i * 16, 16), 16)
        v = acts_v[rows, :].astype(F32)
        m = jnp.mean(v, axis=1, keepdims=True)
        v = v - m
        r = lax.rsqrt(jnp.mean(v * v, axis=1, keepdims=True) + 1e-06)
        lane = lax.broadcasted_iota(jnp.int32, (16, 128), 1)
        rm[rows, :] = jnp.where(lane == 0, r, jnp.where(lane == 1, m, 0.0))
        return 0

    lax.fori_loop(0, 8, stats, 0)
    turned = rm[...].T[:8, :]
    row = lax.broadcasted_iota(jnp.int32, (8, 128), 0)
    st[...] = jnp.where(row == 2, ids_f, turned)
    st_b[g] = st[...]

    stage(1, 0)
    stage(0, 1)

    blocks = []
    for k in range(1, 16):
        cols = pl.ds(pl.multiple_of(me.band(k) * 256, 256), 256)
        cp = remote(acts.at[:, cols], acts_b.at[g], ac_s.at[k], ac_r.at[k], me.mate(k))
        cp.start()
        blocks.append(cp)

    for k in range(1, 16):
        cp = remote(st, st_b.at[g], st_s.at[k], st_r.at[k], me.mate(k))
        cp.start()
        blocks.append(cp)

    loads[3].wait()
    hot_b = hot[:64].astype(BF16)
    for j in range(0, 2048, 512):
        cols = slice(j, j + 512)
        hi, lo = two_terms(og_v[:, cols].astype(F32) * sp_v[:, cols].astype(F32))
        gm[:, cols] = (dot(hot_b, hi, ((1,), (0,))) + dot(hot_b, lo, ((1,), (0,)))).astype(BF16)
    for k in range(16):
        gm_o[me.slot(k)] = gm[:, pl.ds(pl.multiple_of(me.band(k) * 128, 128), 128)]
    swap = remote(gm_o.at[pl.ds(8 - 8 * c, 8)], gm_i, gm_s.at[0], gm_r.at[0], sib)
    swap.start()

    stage(2, 0)
    stage(1, 1)

    @pl.when(takes_half == 1)
    def _():
        half_far.wait_recv()
        half_twin.start()

    stage(2, 1)

    loads[5].wait()

    def scales(j, _):
        cols = pl.ds(pl.multiple_of(j * 512, 512), 512)
        hi, lo = two_terms(ss_v[:, 1, cols])
        sc1[:, cols] = 1.0 + (dot(hot_t, hi, ((1,), (0,))) + dot(hot_t, lo, ((1,), (0,))))
        return 0

    lax.fori_loop(0, 8, scales, 0)

    loads[4].wait()
    loads[6].wait()
    for cp in blocks:
        cp.wait_recv()
    shift_hi, shift_lo = two_terms(ss_b[:, 0, :])
    scale_hi, scale_lo = two_terms(ss_b[:, 1, :])
    tables = jnp.concatenate(
        [
            jnp.concatenate([shift_hi, scale_hi], axis=1),
            jnp.concatenate([shift_lo, scale_lo], axis=1),
        ],
        axis=0,
    )

    def modulate(t, _):
        block = st_b[t]
        wide = jnp.concatenate([block, jnp.zeros((120, 128), F32)], axis=0).T
        r, m = wide[:, 0:1], wide[:, 1:2]
        own = image_hot(block[2:3], 64)
        twice = jnp.concatenate([own, own], axis=0).T.astype(BF16)
        mods = dot(twice, tables, ((1,), (0,)))
        normed = (acts_b[t].astype(F32) - m) * r
        nrm[t] = normed
        out = normed * (1.0 + mods[:, 256:]) + mods[:, :256]
        hid[:, pl.ds(pl.multiple_of(t * 128, 128), 128)] = out.T.astype(BF16)
        rows = lax.broadcasted_iota(jnp.int32, (128, 128), 0)
        hit = ((rows // 2).astype(F32) == block[2:3])
        o2[:, pl.ds(pl.multiple_of(t * 128, 128), 128)] = jnp.where(
            hit & (rows % 2 == 0), 1.0, 0.0
        ).astype(BF16)
        o2[:, pl.ds(pl.multiple_of(2048 + t * 128, 128), 128)] = jnp.where(
            hit & (rows % 2 == 1), 1.0, 0.0
        ).astype(BF16)
        return 0

    lax.fori_loop(0, 16, modulate, 0)

    swap.wait_recv()
    gm_t[...] = (gm_o[pl.ds(8 * c, 8)].astype(F32) + gm_i[...].astype(F32)).astype(BF16)
    gm_b[octet] = gm_t[octet]
    gates = []
    for k in range(1, 8):
        cp = remote(
            gm_t.at[me.slot(k) - 8 * c], gm_b.at[octet], gm_s.at[k], gm_r.at[k], me.mate(k)
        )
        cp.start()
        gates.append(cp)

    parts, first = [], []

    def arrive(half):
        for n in range(3 * half, 3 * half + 3):
            at, width, _ = CHUNKS[n]
            copies[n, 2].wait_recv()
            slots = own_core(7, at, width)
            cp = remote(slots, slots, core_s.at[n], core_r.at[n], sib)
            cp.start()
            copies[n, 3] = cp

    def complete(half):
        for n in range(3 * half, 3 * half + 3):
            copies[n, 3].wait_recv()

    def give(pieces, into, ss_, rs_):
        for k, (piece, to) in enumerate(pieces):
            cp = remote(piece, into, ss_.at[k], rs_.at[q], to)
            if k == 0:
                keep = pltpu.make_async_copy(piece, into, rs_.at[q])
                first.append(cp)

                @pl.when(mine == 0)
                def _():
                    cp.start()

                @pl.when(mine == 1)
                def _():
                    keep.start()

            else:
                cp.start()
                parts.append(cp)

    def give_rows(msg, part, half):
        pieces = [(msg.at[pl.ds(i, 2)], to) for i, to in me.near_holders(b)]
        give(pieces, part.at[q], mw_s.at[half], mw_r.at[half])

    def weight_grad(msg, half):
        def grads(j, _):
            cols = pl.ds(pl.multiple_of(half * SPLIT + j * 256, 256), 256)
            v = dot(hid[...], dz_all[:, :, :, :, cols].reshape(2048, 256), ((1,), (0,)))
            cols = pl.ds(pl.multiple_of(j * 256, 256), 256)
            msg[:, :, cols] = v.astype(BF16).reshape(16, 16, 256)
            return 0

        lax.fori_loop(0, WIDE[half] // 256, grads, 0)

    def back(half):
        lo, hi = half * SPLIT, half * SPLIT + WIDE[half]

        def some(t, _):
            rows = pl.ds(t * 4, 4)
            v = dot(
                dz_all[t, :, :, :, lo:hi].reshape(512, hi - lo),
                w_b[:, lo:hi],
                ((1,), (1,)),
            ).reshape(4, 128, 256)
            if half == 0:
                dh[rows] = v
            else:
                v = v + dh[rows]
                dh_b[rows] = v.astype(BF16)
                v2[rows] = (v * nrm[rows]).astype(BF16)
            return 0

        lax.fori_loop(0, 4, some, 0)

    arrive(0)
    complete(0)
    weight_grad(msg_a, 0)
    give_rows(msg_a, part_a, 0)
    arrive(1)

    @pl.when(takes_half == 1)
    def _():
        half_twin.wait_recv()

    @pl.when(takes_half == 0)
    def _():
        to_far.wait_recv()

    back(0)
    for cp in gates[:7]:
        cp.wait_recv()
    gate_sum = gm_b[0].astype(F32)
    for t in range(1, 8):
        gate_sum = gate_sum + gm_b[t].astype(F32)
    at_row = lax.broadcasted_iota(jnp.int32, (256, 64), 0)
    image = lax.broadcasted_iota(jnp.int32, (256, 64), 1)
    put = (at_row % 16 < 4) & (image == at_row // 16 * 4 + at_row % 16)
    spaced = dot(
        jnp.where(put, 1.0, 0.0).astype(BF16), gate_sum.astype(BF16), ((1,), (0,))
    ).astype(BF16)
    msg_s[:, 1] = spaced.reshape(16, 16, 128)
    complete(1)
    back(1)

    sums = dot(o2[:, :2048], dh_b[...].reshape(2048, 256), ((1,), (0,)))
    sums = sums + dot(o2[:, 2048:], v2[...].reshape(2048, 256), ((1,), (0,)))
    for i in range(16):
        rows = slice(8 * i, 8 * i + 8)
        both = jnp.concatenate([sums[rows, :128], sums[rows, 128:]], axis=0)
        msg_s[i, 0] = both.astype(BF16)


    give([(msg_s.at[i], to) for i, to in me.holders(b)], part_s.at[q], ms_s, ms_r)
    dh_full[:, band_cols] = dh_b[g]
    for k in range(1, 16):
        cp = remote(
            dh_b.at[me.slot(k)], dh_full.at[:, band_cols], dh_s.at[k], dh_r.at[k], me.mate(k)
        )
        cp.start()
        gates.append(cp)
    weight_grad(msg_b, 1)
    give_rows(msg_b, part_b, 1)

    comes = (1 - me.e0, me.zb, 1 - me.e0, 1 - me.zb)

    def collect(part, half):
        wide = WIDE[half]
        acc[...] = jnp.zeros_like(acc)
        for kz in range(4):

            @pl.when(comes[kz] == 1)
            def _():
                for k in range(4):
                    at = 4 * me.zs[kz] + k
                    pltpu.make_async_copy(part.at[at], part.at[at], mw_r.at[half, at]).wait()
                total = part[4 * me.zs[kz]].astype(F32)
                for k in range(1, 4):
                    total = total + part[4 * me.zs[kz] + k].astype(F32)
                acc[:, :, :wide] += total

        to_z[half] = acc[1 - me.zb].astype(BF16)
        at_z[half] = acc[me.zb]
        cp = remote(
            to_z.at[half, :, pl.ds(0, wide)], from_z.at[half, :, pl.ds(0, wide)], tz_s.at[half], tz_r.at[half], me.mate(4),
        )
        cp.start()
        return cp

    for k in range(16):
        pltpu.make_async_copy(part_s.at[k], part_s.at[k], ms_r.at[k]).wait()
    total = part_s[0].astype(F32)
    for k in range(1, 16):
        total = total + part_s[k].astype(F32)
    s_own[...] = (total * MEAN_IMG ** (-0.5)).astype(BF16)
    s1[kept] = s_own[...]
    firsts = []
    for k, to in enumerate(plane):
        cp = remote(s_own, s1.at[kept], s1_s.at[k], s1_r.at[k], to)
        cp.start()
        firsts.append(cp)

    def finish(i, _):
        rows = pl.ds(pl.multiple_of(i * 16, 16), 16)
        r, m = rm[rows, 0:1], rm[rows, 1:2]
        normed = (acts_v[rows, :].astype(F32) - m) * r
        dn = dh_full[rows, :].astype(F32) * sc1[rows, :]
        mean = jnp.mean(dn, axis=1, keepdims=True)
        along = jnp.mean(dn * normed, axis=1, keepdims=True)
        ga[rows, :] = (r * (dn - mean - normed * along)).astype(BF16)
        return 0

    zed = [collect(part_a, 0)]
    rest, own_w, w_line = [], [], []

    def send_rows(half):
        zed[half].wait_recv()
        total = at_z[half] + from_z[half].astype(F32)
        cols = slice(half * SPLIT, half * SPLIT + WIDE[half])
        wp[:, cols] = (total[:, : WIDE[half]] * 32768 ** (-0.5)).astype(BF16)
        piece, into = wp.at[:, cols], o_w.at[h, :, cols]
        own_w.append(pltpu.make_async_copy(piece, into, loc.at[3 + half]))
        own_w[half].start()
        for k, to in enumerate(line):
            cp = remote(piece, into, wp_s.at[half, k], wp_r.at[half, k], to)
            cp.start()
            w_line.append(cp)

    send_rows(0)
    for cp in firsts:
        cp.wait_recv()
    rec[:16] = s1[:, 0]
    rec[16:] = (
        jnp.concatenate([s1[k, 1].astype(F32)[:4] for k in range(16)], axis=0)
        .astype(BF16)
        .reshape(4, 16, 128)
    )
    own_rec = pltpu.make_async_copy(rec, o_rec.at[h], loc.at[1])
    own_rec.start()
    for k, to in enumerate(line):
        cp = remote(rec, o_rec.at[h], sm_s.at[k], sm_r.at[k], to)
        cp.start()
        rest.append(cp)
    zed.append(collect(part_b, 1))
    send_rows(1)
    for cp in gates[7:]:
        cp.wait_recv()

    lax.fori_loop(0, 8, finish, 0)
    out = pltpu.make_async_copy(ga, o_acts, loc.at[2])
    out.start()

    mates = pl.ds(c * 8, 8)
    last = []
    own_rec.wait()
    for cp in own_w:
        cp.wait()
    for i, (v, sent) in enumerate(((o_rec, rest), (o_w, w_line))):
        for cp in sent:
            cp.wait_recv()
        cp = remote(v.at[mates], v.at[mates], co_s.at[i], co_r.at[i], sib)
        cp.start()
        last.append(cp)
    last[0].wait_recv()
    last[1].wait_recv()
    out.wait()
    for cp in copies.values():
        cp.wait_send()
    for cp in blocks + [swap] + gates + parts + firsts + rest + w_line + last + zed:
        cp.wait_send()

    @pl.when(mine == 0)
    def _():
        for cp in first:
            cp.wait_send()

    @pl.when(c == 1)
    def _():
        to_far.wait_send()

    @pl.when((1 - c) * me.e == 1)
    def _():
        half_far.wait_send()

    @pl.when(takes_half == 1)
    def _():
        half_twin.wait_send()

    @pl.when(swaps == 1)
    def _():
        to_near.wait_send()


def lay_out_kernel(acts, w, rec_in, o_acts, o_w, o_mod, o_gate, rec, mod, gate, va, vw, sem):
    fetch = [
        pltpu.make_async_copy(a, v, sem.at[i])
        for i, (a, v) in enumerate(((rec_in, rec), (acts, va), (w, vw)))
    ]
    for cp in fetch:
        cp.start()
    fetch[0].wait()
    sent = []

    def write(i, _):
        images = pl.ds(i * 4, 4)
        for k in range(16):
            v = rec[i, k].astype(F32)
            mod[images, :, k * 256 : k * 256 + 128] = v[:8].reshape(4, 2, 128)
            mod[images, :, k * 256 + 128 : k * 256 + 256] = v[8:].reshape(4, 2, 128)
        return 0

    for half in range(2):
        lax.fori_loop(8 * half, 8 * half + 8, write, 0)
        images = pl.ds(32 * half, 32)
        cp = pltpu.make_async_copy(mod.at[images], o_mod.at[images], sem.at[3 + half])
        cp.start()
        sent.append(cp)
        fetch[1 + half].wait()
        v, o = ((va, o_acts), (vw, o_w))[half]
        cp = pltpu.make_async_copy(v, o, sem.at[5 + half])
        cp.start()
        sent.append(cp)
    for i in range(16):
        v = rec[i, 16:].reshape(64, 128).astype(F32)
        for k in range(16):
            gate[4 * i : 4 * i + 4, k * 128 : k * 128 + 128] = v[4 * k : 4 * k + 4]
    cp = pltpu.make_async_copy(gate, o_gate, sem.at[7])
    cp.start()
    sent.append(cp)
    for cp in sent:
        cp.wait()


def on_device(acts, out_grad, saved_proj, weight, shift_scale, gate, image_of):
    n = len(CHUNKS)
    dma = pltpu.SemaphoreType.DMA
    hbm = pl.BlockSpec(memory_space=pl.ANY)
    local = pl.BlockSpec(memory_space=pltpu.VMEM)
    vmem = pltpu.VMEM
    mid_acts, mid_w, mid_rec = pl.pallas_call(
        block_kernel,
        out_shape=(
            jax.ShapeDtypeStruct((128, 4096), BF16),
            jax.ShapeDtypeStruct((16, 16, 2048), BF16),
            jax.ShapeDtypeStruct((16, 20, 16, 128), BF16),
        ),
        in_specs=[pl.BlockSpec(memory_space=pltpu.HBM)] * 6 + [local],
        out_specs=(hbm, hbm, hbm),
        scratch_shapes=[
            vmem((128, 4096), BF16), vmem((128, 2048), BF16), vmem((128, 2048), BF16),
            vmem((64, 2048), F32), vmem((64, 2, 4096), F32), vmem((64, 2, 256), F32),
            vmem((128, 128), F32), vmem((8, 128), F32), vmem((4, 2, 2, 128, 2048), BF16),
            vmem((16, 128, 256), BF16), vmem((16, 8, 128), F32),
            vmem((64, 2048), BF16), vmem((16, 64, 128), BF16), vmem((8, 64, 128), BF16),
            vmem((8, 64, 128), BF16), vmem((8, 64, 128), BF16), vmem((256, 2048), BF16),
            vmem((256, 2048), BF16), vmem((16, 128, 256), F32), vmem((16, 128, 256), F32),
            vmem((16, 128, 256), BF16), vmem((16, 16, SPLIT), BF16), vmem((16, 16, WIDE[1]), BF16),
            vmem((16, 2, 16, 128), BF16), vmem((16, 2, 16, SPLIT), BF16),
            vmem((16, 2, 16, WIDE[1]), BF16), vmem((16, 2, 16, 128), BF16),
            vmem((128, 4096), BF16), vmem((128, 4096), F32), vmem((16, 2048), BF16),
            vmem((2, 16, 128), BF16), vmem((16, 2, 16, 128), BF16),
            vmem((20, 16, 128), BF16), vmem((128, 4096), BF16), vmem((128, 4096), BF16),
            vmem((16, 128, 256), BF16),
            vmem((2, 16, max(WIDE)), F32), vmem((2, 16, max(WIDE)), BF16),
            vmem((2, 16, max(WIDE)), BF16), vmem((2, 16, max(WIDE)), F32),
            dma((n, 3)), dma((n, 3)), dma((n,)), dma((n,)),
            dma((16,)), dma((16,)), dma((16,)), dma((16,)), dma((8,)), dma((8,)),
            dma((4,)), dma((3,)), dma((16,)), dma((16,)), dma((2, 8)), dma((2, 16)),
            dma((16,)), dma((16,)), dma((15,)), dma((15,)), dma((2, 7)), dma((2, 7)), dma((7,)), dma((7,)),
            dma((2,)), dma((2,)), dma((2,)), dma((2,)), dma((7,)),
        ],
        compiler_params=pltpu.CompilerParams(
            collective_id=0, has_side_effects=True, vmem_limit_bytes=60 * 2**20
        ),
        name="adaln_backward",
    )(acts, out_grad, saved_proj, weight, shift_scale, gate, image_of.reshape(1, 128))
    o_acts, o_w, o_mod, o_gate = pl.pallas_call(
        lay_out_kernel,
        out_shape=(
            jax.ShapeDtypeStruct((128, 4096), BF16),
            jax.ShapeDtypeStruct((16, 16, 2048), BF16),
            jax.ShapeDtypeStruct((64, 2, 4096), F32),
            jax.ShapeDtypeStruct((64, 2048), F32),
        ),
        in_specs=[hbm, hbm, hbm],
        out_specs=(hbm, hbm, hbm, hbm),
        scratch_shapes=[
            vmem((16, 20, 16, 128), BF16), vmem((64, 2, 4096), F32), vmem((64, 2048), F32),
            vmem((128, 4096), BF16), vmem((16, 16, 2048), BF16), dma((10,)),
        ],
        compiler_params=pltpu.CompilerParams(vmem_limit_bytes=60 * 2**20),
        name="lay_out",
    )(mid_acts, mid_w, mid_rec)
    return o_acts, o_w.reshape(256, 2048), o_mod, o_gate


def solution(mesh):
    placed = (
        P(("rep", "shard"), None),
        P(("rep", "shard"), None),
        P(("rep", "shard"), None),
        P("shard", None),
        P(),
        P(),
        P(("rep", "shard")),
    )
    return jax.shard_map(
        on_device,
        mesh=mesh,
        in_specs=placed,
        out_specs=(P(("rep", "shard"), None), P("shard", None), P(), P()),
        check_vma=False,
    )
```

```python
import jax
import jax.numpy as jnp
from jax import lax
from jax.experimental import pallas as pl
from jax.experimental.pallas import tpu as pltpu
from jax.sharding import PartitionSpec as P

MEAN_IMG = 512
MESH = pl.DeviceIdType.MESH
BF16 = jnp.bfloat16
F32 = jnp.float32
CHUNKS = (
    (0, 128, (0, 1, 2)),
    (128, 256, (1, 2, 0)),
    (384, 384, (2, 0, 1)),
    (768, 384, (0, 1, 2)),
    (1152, 512, (1, 2, 0)),
    (1664, 384, (2, 0, 1)),
)
SPLIT = 768
WIDE = (768, 1280)


def signal(at):
    pl.semaphore_signal(
        pltpu.get_barrier_semaphore(), inc=1, device_id=at, device_id_type=MESH
    )


def remote(src, dst, ss, rs, at):
    return pltpu.make_async_remote_copy(
        src_ref=src,
        dst_ref=dst,
        send_sem=ss,
        recv_sem=rs,
        device_id=at,
        device_id_type=MESH,
    )


class Place:
    def __init__(self):
        r, s = lax.axis_index("rep"), lax.axis_index("shard")
        self.r, self.s = r, s
        self.zb, self.x, self.c = lax.div(r, 8), lax.rem(lax.div(r, 2), 4), lax.rem(r, 2)
        self.y, self.zh = lax.div(s, 4), lax.rem(s, 4)
        self.xb, self.yb = lax.rem(self.x, 2), lax.rem(self.y, 2)
        self.xh, self.yh = lax.div(self.x, 2), lax.div(self.y, 2)
        self.odd = lax.rem(self.zh, 2)
        bits = (self.xb, self.yb, self.zb, self.c)
        self.turn = [1 - 2 * b for b in bits]
        self.slot0 = self.xb + 2 * self.yb + 4 * self.zb + 8 * self.c
        p = lax.rem(self.xb + self.c, 2)
        e = lax.rem(self.zb + self.odd, 2)
        self.p, self.e = p, e
        self.e0 = 1 - e
        ys = (self.y, self.y + self.turn[1])
        self.band_y = [[v + w * (3 - 2 * v) for w in (p, 1 - p)] for v in ys]
        self.band_z = []
        for kz in range(2):
            zb, ev = (1 - self.zb, 1 - e) if kz else (self.zb, e)
            row = []
            for kc in range(2):
                c = 1 - self.c if kc else self.c
                row.append(lax.rem(self.zh + c * (2 * zb + 3) + (1 - c) * 2 * (1 - ev), 4))
            self.band_z.append(row)
        self.xs = [lax.rem(self.x + k, 4) for k in range(4)]
        self.ys = [lax.rem(self.y + k, 4) * 4 for k in range(4)]
        self.zs = [lax.rem(self.zh + k, 4) for k in range(4)]

    def mate(self, k):
        r = self.r
        for bit, step in ((0, 2), (2, 8), (3, 1)):
            if k >> bit & 1:
                r = r + step * self.turn[bit]
        return r, self.s + 4 * self.turn[1] if k & 2 else self.s

    def slot(self, k):
        v = self.slot0
        for bit in range(4):
            if k >> bit & 1:
                v = v + (1 << bit) * self.turn[bit]
        return v

    def band(self, k):
        kx, ky, kz, kc = (k >> i & 1 for i in range(4))
        return 4 * self.band_y[ky][kx ^ kc] + self.band_z[kz][kc]

    def far(self):
        z = 2 * self.zh + self.zb + (2 * self.zb - 1) * (3 - 2 * self.c) + 8
        y = self.y + self.p * (3 - 2 * self.y)
        return lax.rem(z, 2) * 8 + self.x * 2 + self.c, y * 4 + lax.rem(lax.div(z, 2), 4)

    def pair(self):
        return self.zb * 8 + (3 - self.x) * 2 + self.c, (3 - self.y) * 4 + self.zh

    def near(self):
        return self.r, (3 - self.y) * 4 + self.zh

    def senders(self):
        found = []
        for k in range(16):
            kx, ky, kz = k % 2, k // 2 % 2, k // 4
            d = (4 - kz) % 4
            c = d % 2
            if c:
                zb = (3 - d) // 2
            else:
                zb = 1 - self.odd if (1 + d // 2 + kz) % 2 else self.odd
            xh = 1 - self.xh if kx else self.xh
            y = 3 - self.y if ky else self.y
            found.append((zb * 8 + (2 * xh + (ky + c) % 2) * 2 + c, y * 4 + self.zs[kz]))
        return found

    def holders(self, band):
        zs, cs = (self.zb, 1 - self.zb), (self.c, 1 - self.c)
        return [
            (
                2 * self.xs[k % 4] + zs[k // 4 % 2] + 8 * cs[k // 8],
                (zs[k // 4 % 2] * 8 + self.xs[k % 4] * 2 + cs[k // 8], band),
            )
            for k in range(16)
        ]

    def near_holders(self, band):
        far = 1 - (1 - self.c) * self.e
        zb = self.zb + self.turn[2] * far
        cs = (self.c, 1 - self.c)
        return [
            (
                2 * self.xs[k % 4] + 8 * cs[k // 4],
                (zb * 8 + self.xs[k % 4] * 2 + cs[k // 4], band),
            )
            for k in range(8)
        ]

    def plane(self):
        return [(self.r, self.ys[k // 4] + self.zs[k % 4]) for k in range(1, 16)]

    def line(self):
        zs = (self.zb, 1 - self.zb)
        return [(zs[k // 4] * 8 + self.xs[k % 4] * 2 + self.c, self.s) for k in range(1, 8)]


def dot(a, b, dims):
    return lax.dot_general(a, b, (dims, ((), ())), preferred_element_type=F32)


def two_terms(v):
    hi = v.astype(BF16)
    return hi, (v - hi.astype(F32)).astype(BF16)


def image_hot(ids, count):
    rows = lax.broadcasted_iota(jnp.int32, (count, ids.shape[1]), 0).astype(F32)
    return jnp.where(rows == ids, 1.0, 0.0)


def block_kernel(
    acts, og, sp, w, ss, gate, ids,
    o_acts, o_w, o_rec,
    acts_v, og_v, sp_v, gate_v, ss_v, ss_b, rm, st, dz_all, acts_b, st_b,
    gm, gm_o, gm_i, gm_t, gm_b, w_b, hid, nrm, dh, dh_b, msg_a, msg_b, msg_s, part_a, part_b, part_s,
    dh_full, sc1, wp, s_own, s1, rec, ga, o2, v2, acc, to_z, from_z, at_z,
    dz_s, dz_r, core_s, core_r, ac_s, ac_r, st_s, st_r, gm_s, gm_r, w_s, w_r,
    dh_s, dh_r, mw_s, mw_r, ms_s, ms_r, s1_s, s1_r, wp_s, wp_r, sm_s, sm_r, co_s, co_r, tz_s, tz_r, loc,
):
    me = Place()
    c, g, b = me.c, me.slot0, me.band(0)
    far, near = me.far(), me.near()
    keeps = (1 - c) * me.e * (1 - me.p)
    swaps = (1 - c) * me.e * me.p
    takes_half = (1 - c) * (1 - me.e)
    pair = me.pair()
    mine = keeps
    q = me.xh + 2 * me.yh + 4 * me.zh
    h = 2 * me.x + me.zb + 8 * c
    kept = me.s
    sib = me.mate(8)
    plane, line = me.plane(), me.line()
    cz = 2 * c + me.zb
    octet = g - 8 * c
    band_cols = pl.ds(pl.multiple_of(b * 256, 256), 256)

    def own_core(bits, at, width):
        return dz_all.at[
            pl.ds(2 * c, 2) if bits & 4 else cz,
            pl.ds(0, 2) if bits & 2 else me.yb,
            pl.ds(0, 2) if bits & 1 else me.xb,
            :,
            pl.ds(at, width),
        ]

    loads = [
        pltpu.make_async_copy(a, v, loc.at[i])
        for i, (a, v) in enumerate(
            ((og, og_v), (gate, gate_v), (acts, acts_v), (sp, sp_v),
             (ss.at[:, :, band_cols], ss_b), (ss, ss_v), (acts.at[:, band_cols], acts_b.at[g]))
        )
    ]
    for cp in loads:
        cp.start()
    for k in range(1, 16):
        signal(me.mate(k))
    signal(far)

    @pl.when(swaps == 1)
    def _():
        signal(near)

    @pl.when(takes_half == 1)
    def _():
        signal(pair)

    senders = me.senders()

    @pl.when(mine == 0)
    def _():
        signal(senders[0])

    for to in senders[1:]:
        signal(to)
    for to in plane + line:
        signal(to)

    ids_f = ids[...].astype(F32)
    hot = image_hot(ids_f, 128)
    hot_t = hot.T[:, :64].astype(BF16)
    loads[0].wait()
    loads[1].wait()
    for j in range(0, 2048, 512):
        cols = slice(j, j + 512)
        hi, lo = two_terms(gate_v[:, cols])
        rows = dot(hot_t, hi, ((1,), (0,))) + dot(hot_t, lo, ((1,), (0,)))
        dz_all[cz, me.yb, me.xb, :, cols] = (rows * og_v[:, cols].astype(F32)).astype(BF16)

    pl.semaphore_wait(pltpu.get_barrier_semaphore(), 54 + swaps + takes_half - mine)

    copies = {}

    def stage(k, half):
        for n in range(3 * half, 3 * half + 3):
            at, width, order = CHUNKS[n]
            if k:
                copies[n, k - 1].wait_recv()
            slots = own_core(sum(1 << d for d in order[:k]), at, width)
            cp = remote(slots, slots, dz_s.at[n, k], dz_r.at[n, k], me.mate(1 << order[k]))
            cp.start()
            copies[n, k] = cp

    stage(0, 0)

    half_rows = pl.ds(pl.multiple_of(128 * lax.div(me.x, 2), 128), 128)
    to_far = remote(w, w_b, w_s.at[0], w_r.at[0], far)
    to_near = remote(w, w_b, w_s.at[1], w_r.at[0], near)
    to_self = pltpu.make_async_copy(w, w_b, w_r.at[0])
    half_far = remote(w.at[half_rows], w_b.at[half_rows], w_s.at[2], w_r.at[1], far)
    half_twin = remote(w_b.at[half_rows], w_b.at[half_rows], w_s.at[3], w_r.at[2], pair)

    @pl.when(c == 1)
    def _():
        to_far.start()

    @pl.when((1 - c) * me.e == 1)
    def _():
        half_far.start()

    @pl.when(swaps == 1)
    def _():
        to_near.start()

    @pl.when(keeps == 1)
    def _():
        to_self.start()

    loads[2].wait()

    def stats(i, _):
        rows = pl.ds(pl.multiple_of(i * 16, 16), 16)
        v = acts_v[rows, :].astype(F32)
        m = jnp.mean(v, axis=1, keepdims=True)
        v = v - m
        r = lax.rsqrt(jnp.mean(v * v, axis=1, keepdims=True) + 1e-06)
        lane = lax.broadcasted_iota(jnp.int32, (16, 128), 1)
        rm[rows, :] = jnp.where(lane == 0, r, jnp.where(lane == 1, m, 0.0))
        return 0

    lax.fori_loop(0, 8, stats, 0)
    turned = rm[...].T[:8, :]
    row = lax.broadcasted_iota(jnp.int32, (8, 128), 0)
    st[...] = jnp.where(row == 2, ids_f, turned)
    st_b[g] = st[...]

    stage(1, 0)
    stage(0, 1)

    blocks = []
    for k in range(1, 16):
        cols = pl.ds(pl.multiple_of(me.band(k) * 256, 256), 256)
        cp = remote(acts.at[:, cols], acts_b.at[g], ac_s.at[k], ac_r.at[k], me.mate(k))
        cp.start()
        blocks.append(cp)

    for k in range(1, 16):
        cp = remote(st, st_b.at[g], st_s.at[k], st_r.at[k], me.mate(k))
        cp.start()
        blocks.append(cp)

    loads[3].wait()
    hot_b = hot[:64].astype(BF16)
    for j in range(0, 2048, 512):
        cols = slice(j, j + 512)
        hi, lo = two_terms(og_v[:, cols].astype(F32) * sp_v[:, cols].astype(F32))
        gm[:, cols] = (dot(hot_b, hi, ((1,), (0,))) + dot(hot_b, lo, ((1,), (0,)))).astype(BF16)
    for k in range(16):
        gm_o[me.slot(k)] = gm[:, pl.ds(pl.multiple_of(me.band(k) * 128, 128), 128)]
    swap = remote(gm_o.at[pl.ds(8 - 8 * c, 8)], gm_i, gm_s.at[0], gm_r.at[0], sib)
    swap.start()

    stage(2, 0)
    stage(1, 1)
    stage(2, 1)

    @pl.when(takes_half == 1)
    def _():
        half_far.wait_recv()
        half_twin.start()

    loads[5].wait()

    def scales(j, _):
        cols = pl.ds(pl.multiple_of(j * 512, 512), 512)
        hi, lo = two_terms(ss_v[:, 1, cols])
        sc1[:, cols] = 1.0 + (dot(hot_t, hi, ((1,), (0,))) + dot(hot_t, lo, ((1,), (0,))))
        return 0

    lax.fori_loop(0, 8, scales, 0)

    loads[4].wait()
    loads[6].wait()
    for cp in blocks:
        cp.wait_recv()
    shift_hi, shift_lo = two_terms(ss_b[:, 0, :])
    scale_hi, scale_lo = two_terms(ss_b[:, 1, :])
    tables = jnp.concatenate(
        [
            jnp.concatenate([shift_hi, scale_hi], axis=1),
            jnp.concatenate([shift_lo, scale_lo], axis=1),
        ],
        axis=0,
    )

    def modulate(t, _):
        block = st_b[t]
        wide = jnp.concatenate([block, jnp.zeros((120, 128), F32)], axis=0).T
        r, m = wide[:, 0:1], wide[:, 1:2]
        own = image_hot(block[2:3], 64)
        twice = jnp.concatenate([own, own], axis=0).T.astype(BF16)
        mods = dot(twice, tables, ((1,), (0,)))
        normed = (acts_b[t].astype(F32) - m) * r
        nrm[t] = normed
        out = normed * (1.0 + mods[:, 256:]) + mods[:, :256]
        hid[:, pl.ds(pl.multiple_of(t * 128, 128), 128)] = out.T.astype(BF16)
        rows = lax.broadcasted_iota(jnp.int32, (128, 128), 0)
        hit = ((rows // 2).astype(F32) == block[2:3])
        o2[:, pl.ds(pl.multiple_of(t * 128, 128), 128)] = jnp.where(
            hit & (rows % 2 == 0), 1.0, 0.0
        ).astype(BF16)
        o2[:, pl.ds(pl.multiple_of(2048 + t * 128, 128), 128)] = jnp.where(
            hit & (rows % 2 == 1), 1.0, 0.0
        ).astype(BF16)
        return 0

    lax.fori_loop(0, 16, modulate, 0)

    swap.wait_recv()
    gm_t[...] = (gm_o[pl.ds(8 * c, 8)].astype(F32) + gm_i[...].astype(F32)).astype(BF16)
    gm_b[octet] = gm_t[octet]
    gates = []
    for k in range(1, 8):
        cp = remote(
            gm_t.at[me.slot(k) - 8 * c], gm_b.at[octet], gm_s.at[k], gm_r.at[k], me.mate(k)
        )
        cp.start()
        gates.append(cp)

    parts, first = [], []

    def arrive(half):
        for n in range(3 * half, 3 * half + 3):
            at, width, _ = CHUNKS[n]
            copies[n, 2].wait_recv()
            slots = own_core(7, at, width)
            cp = remote(slots, slots, core_s.at[n], core_r.at[n], sib)
            cp.start()
            copies[n, 3] = cp

    def complete(half):
        for n in range(3 * half, 3 * half + 3):
            copies[n, 3].wait_recv()

    def give(pieces, into, ss_, rs_):
        for k, (piece, to) in enumerate(pieces):
            cp = remote(piece, into, ss_.at[k], rs_.at[q], to)
            if k == 0:
                keep = pltpu.make_async_copy(piece, into, rs_.at[q])
                first.append(cp)

                @pl.when(mine == 0)
                def _():
                    cp.start()

                @pl.when(mine == 1)
                def _():
                    keep.start()

            else:
                cp.start()
                parts.append(cp)

    def give_rows(msg, part, half):
        pieces = [(msg.at[pl.ds(i, 2)], to) for i, to in me.near_holders(b)]
        give(pieces, part.at[q], mw_s.at[half], mw_r.at[half])

    def weight_grad(msg, half):
        def grads(j, _):
            cols = pl.ds(pl.multiple_of(half * SPLIT + j * 256, 256), 256)
            v = dot(hid[...], dz_all[:, :, :, :, cols].reshape(2048, 256), ((1,), (0,)))
            cols = pl.ds(pl.multiple_of(j * 256, 256), 256)
            msg[:, :, cols] = v.astype(BF16).reshape(16, 16, 256)
            return 0

        lax.fori_loop(0, WIDE[half] // 256, grads, 0)

    def back(half):
        lo, hi = half * SPLIT, half * SPLIT + WIDE[half]

        def some(t, _):
            rows = pl.ds(t * 4, 4)
            v = dot(
                dz_all[t, :, :, :, lo:hi].reshape(512, hi - lo),
                w_b[:, lo:hi],
                ((1,), (1,)),
            ).reshape(4, 128, 256)
            if half == 0:
                dh[rows] = v
            else:
                v = v + dh[rows]
                dh_b[rows] = v.astype(BF16)
                v2[rows] = (v * nrm[rows]).astype(BF16)
            return 0

        lax.fori_loop(0, 4, some, 0)

    arrive(0)
    complete(0)
    weight_grad(msg_a, 0)
    give_rows(msg_a, part_a, 0)
    arrive(1)

    @pl.when(takes_half == 1)
    def _():
        half_twin.wait_recv()

    @pl.when(takes_half == 0)
    def _():
        to_far.wait_recv()

    back(0)
    for cp in gates[:7]:
        cp.wait_recv()
    gate_sum = gm_b[0].astype(F32)
    for t in range(1, 8):
        gate_sum = gate_sum + gm_b[t].astype(F32)
    at_row = lax.broadcasted_iota(jnp.int32, (256, 64), 0)
    image = lax.broadcasted_iota(jnp.int32, (256, 64), 1)
    put = (at_row % 16 < 4) & (image == at_row // 16 * 4 + at_row % 16)
    spaced = dot(
        jnp.where(put, 1.0, 0.0).astype(BF16), gate_sum.astype(BF16), ((1,), (0,))
    ).astype(BF16)
    msg_s[:, 1] = spaced.reshape(16, 16, 128)
    complete(1)
    back(1)

    sums = dot(o2[:, :2048], dh_b[...].reshape(2048, 256), ((1,), (0,)))
    sums = sums + dot(o2[:, 2048:], v2[...].reshape(2048, 256), ((1,), (0,)))
    for i in range(16):
        rows = slice(8 * i, 8 * i + 8)
        both = jnp.concatenate([sums[rows, :128], sums[rows, 128:]], axis=0)
        msg_s[i, 0] = both.astype(BF16)


    give([(msg_s.at[i], to) for i, to in me.holders(b)], part_s.at[q], ms_s, ms_r)
    dh_full[:, band_cols] = dh_b[g]
    for k in range(1, 16):
        cp = remote(
            dh_b.at[me.slot(k)], dh_full.at[:, band_cols], dh_s.at[k], dh_r.at[k], me.mate(k)
        )
        cp.start()
        gates.append(cp)
    weight_grad(msg_b, 1)
    give_rows(msg_b, part_b, 1)

    comes = (1 - me.e0, me.zb, 1 - me.e0, 1 - me.zb)

    def collect(part, half):
        wide = WIDE[half]
        acc[...] = jnp.zeros_like(acc)
        for kz in range(4):

            @pl.when(comes[kz] == 1)
            def _():
                for k in range(4):
                    at = 4 * me.zs[kz] + k
                    pltpu.make_async_copy(part.at[at], part.at[at], mw_r.at[half, at]).wait()
                total = part[4 * me.zs[kz]].astype(F32)
                for k in range(1, 4):
                    total = total + part[4 * me.zs[kz] + k].astype(F32)
                acc[:, :, :wide] += total

        to_z[half] = acc[1 - me.zb].astype(BF16)
        at_z[half] = acc[me.zb]
        cp = remote(
            to_z.at[half, :, pl.ds(0, wide)], from_z.at[half, :, pl.ds(0, wide)], tz_s.at[half], tz_r.at[half], me.mate(4),
        )
        cp.start()
        return cp

    for k in range(16):
        pltpu.make_async_copy(part_s.at[k], part_s.at[k], ms_r.at[k]).wait()
    total = part_s[0].astype(F32)
    for k in range(1, 16):
        total = total + part_s[k].astype(F32)
    s_own[...] = (total * MEAN_IMG ** (-0.5)).astype(BF16)
    s1[kept] = s_own[...]
    firsts = []
    for k, to in enumerate(plane):
        cp = remote(s_own, s1.at[kept], s1_s.at[k], s1_r.at[k], to)
        cp.start()
        firsts.append(cp)

    def finish(i, _):
        rows = pl.ds(pl.multiple_of(i * 16, 16), 16)
        r, m = rm[rows, 0:1], rm[rows, 1:2]
        normed = (acts_v[rows, :].astype(F32) - m) * r
        dn = dh_full[rows, :].astype(F32) * sc1[rows, :]
        mean = jnp.mean(dn, axis=1, keepdims=True)
        along = jnp.mean(dn * normed, axis=1, keepdims=True)
        ga[rows, :] = (r * (dn - mean - normed * along)).astype(BF16)
        return 0

    zed = [collect(part_a, 0)]
    rest, own_w, w_line = [], [], []

    def send_rows(half):
        zed[half].wait_recv()
        total = at_z[half] + from_z[half].astype(F32)
        cols = slice(half * SPLIT, half * SPLIT + WIDE[half])
        wp[:, cols] = (total[:, : WIDE[half]] * 32768 ** (-0.5)).astype(BF16)
        piece, into = wp.at[:, cols], o_w.at[h, :, cols]
        own_w.append(pltpu.make_async_copy(piece, into, loc.at[3 + half]))
        own_w[half].start()
        for k, to in enumerate(line):
            cp = remote(piece, into, wp_s.at[half, k], wp_r.at[half, k], to)
            cp.start()
            w_line.append(cp)

    send_rows(0)
    for cp in firsts:
        cp.wait_recv()
    rec[:16] = s1[:, 0]
    rec[16:] = (
        jnp.concatenate([s1[k, 1].astype(F32)[:4] for k in range(16)], axis=0)
        .astype(BF16)
        .reshape(4, 16, 128)
    )
    own_rec = pltpu.make_async_copy(rec, o_rec.at[h], loc.at[1])
    own_rec.start()
    for k, to in enumerate(line):
        cp = remote(rec, o_rec.at[h], sm_s.at[k], sm_r.at[k], to)
        cp.start()
        rest.append(cp)
    zed.append(collect(part_b, 1))
    send_rows(1)
    for cp in gates[7:]:
        cp.wait_recv()

    lax.fori_loop(0, 8, finish, 0)
    out = pltpu.make_async_copy(ga, o_acts, loc.at[2])
    out.start()

    mates = pl.ds(c * 8, 8)
    last = []
    own_rec.wait()
    for cp in own_w:
        cp.wait()
    for i, (v, sent) in enumerate(((o_rec, rest), (o_w, w_line))):
        for cp in sent:
            cp.wait_recv()
        cp = remote(v.at[mates], v.at[mates], co_s.at[i], co_r.at[i], sib)
        cp.start()
        last.append(cp)
    last[0].wait_recv()
    last[1].wait_recv()
    out.wait()
    for cp in copies.values():
        cp.wait_send()
    for cp in blocks + [swap] + gates + parts + firsts + rest + w_line + last + zed:
        cp.wait_send()

    @pl.when(mine == 0)
    def _():
        for cp in first:
            cp.wait_send()

    @pl.when(c == 1)
    def _():
        to_far.wait_send()

    @pl.when((1 - c) * me.e == 1)
    def _():
        half_far.wait_send()

    @pl.when(takes_half == 1)
    def _():
        half_twin.wait_send()

    @pl.when(swaps == 1)
    def _():
        to_near.wait_send()


def lay_out_kernel(acts, w, rec_in, o_acts, o_w, o_mod, o_gate, rec, mod, gate, va, vw, sem):
    fetch = [
        pltpu.make_async_copy(a, v, sem.at[i])
        for i, (a, v) in enumerate(((rec_in, rec), (acts, va), (w, vw)))
    ]
    for cp in fetch:
        cp.start()
    fetch[0].wait()
    sent = []

    def write(i, _):
        images = pl.ds(i * 4, 4)
        for k in range(16):
            v = rec[i, k].astype(F32)
            mod[images, :, k * 256 : k * 256 + 128] = v[:8].reshape(4, 2, 128)
            mod[images, :, k * 256 + 128 : k * 256 + 256] = v[8:].reshape(4, 2, 128)
        return 0

    for half in range(2):
        lax.fori_loop(8 * half, 8 * half + 8, write, 0)
        images = pl.ds(32 * half, 32)
        cp = pltpu.make_async_copy(mod.at[images], o_mod.at[images], sem.at[3 + half])
        cp.start()
        sent.append(cp)
        fetch[1 + half].wait()
        v, o = ((va, o_acts), (vw, o_w))[half]
        cp = pltpu.make_async_copy(v, o, sem.at[5 + half])
        cp.start()
        sent.append(cp)
    for i in range(16):
        v = rec[i, 16:].reshape(64, 128).astype(F32)
        for k in range(16):
            gate[4 * i : 4 * i + 4, k * 128 : k * 128 + 128] = v[4 * k : 4 * k + 4]
    cp = pltpu.make_async_copy(gate, o_gate, sem.at[7])
    cp.start()
    sent.append(cp)
    for cp in sent:
        cp.wait()


def on_device(acts, out_grad, saved_proj, weight, shift_scale, gate, image_of):
    n = len(CHUNKS)
    dma = pltpu.SemaphoreType.DMA
    hbm = pl.BlockSpec(memory_space=pl.ANY)
    local = pl.BlockSpec(memory_space=pltpu.VMEM)
    vmem = pltpu.VMEM
    mid_acts, mid_w, mid_rec = pl.pallas_call(
        block_kernel,
        out_shape=(
            jax.ShapeDtypeStruct((128, 4096), BF16),
            jax.ShapeDtypeStruct((16, 16, 2048), BF16),
            jax.ShapeDtypeStruct((16, 20, 16, 128), BF16),
        ),
        in_specs=[pl.BlockSpec(memory_space=pltpu.HBM)] * 6 + [local],
        out_specs=(hbm, hbm, hbm),
        scratch_shapes=[
            vmem((128, 4096), BF16), vmem((128, 2048), BF16), vmem((128, 2048), BF16),
            vmem((64, 2048), F32), vmem((64, 2, 4096), F32), vmem((64, 2, 256), F32),
            vmem((128, 128), F32), vmem((8, 128), F32), vmem((4, 2, 2, 128, 2048), BF16),
            vmem((16, 128, 256), BF16), vmem((16, 8, 128), F32),
            vmem((64, 2048), BF16), vmem((16, 64, 128), BF16), vmem((8, 64, 128), BF16),
            vmem((8, 64, 128), BF16), vmem((8, 64, 128), BF16), vmem((256, 2048), BF16),
            vmem((256, 2048), BF16), vmem((16, 128, 256), F32), vmem((16, 128, 256), F32),
            vmem((16, 128, 256), BF16), vmem((16, 16, SPLIT), BF16), vmem((16, 16, WIDE[1]), BF16),
            vmem((16, 2, 16, 128), BF16), vmem((16, 2, 16, SPLIT), BF16),
            vmem((16, 2, 16, WIDE[1]), BF16), vmem((16, 2, 16, 128), BF16),
            vmem((128, 4096), BF16), vmem((128, 4096), F32), vmem((16, 2048), BF16),
            vmem((2, 16, 128), BF16), vmem((16, 2, 16, 128), BF16),
            vmem((20, 16, 128), BF16), vmem((128, 4096), BF16), vmem((128, 4096), BF16),
            vmem((16, 128, 256), BF16),
            vmem((2, 16, max(WIDE)), F32), vmem((2, 16, max(WIDE)), BF16),
            vmem((2, 16, max(WIDE)), BF16), vmem((2, 16, max(WIDE)), F32),
            dma((n, 3)), dma((n, 3)), dma((n,)), dma((n,)),
            dma((16,)), dma((16,)), dma((16,)), dma((16,)), dma((8,)), dma((8,)),
            dma((4,)), dma((3,)), dma((16,)), dma((16,)), dma((2, 8)), dma((2, 16)),
            dma((16,)), dma((16,)), dma((15,)), dma((15,)), dma((2, 7)), dma((2, 7)), dma((7,)), dma((7,)),
            dma((2,)), dma((2,)), dma((2,)), dma((2,)), dma((7,)),
        ],
        compiler_params=pltpu.CompilerParams(
            collective_id=0, has_side_effects=True, vmem_limit_bytes=60 * 2**20
        ),
        name="adaln_backward",
    )(acts, out_grad, saved_proj, weight, shift_scale, gate, image_of.reshape(1, 128))
    o_acts, o_w, o_mod, o_gate = pl.pallas_call(
        lay_out_kernel,
        out_shape=(
            jax.ShapeDtypeStruct((128, 4096), BF16),
            jax.ShapeDtypeStruct((16, 16, 2048), BF16),
            jax.ShapeDtypeStruct((64, 2, 4096), F32),
            jax.ShapeDtypeStruct((64, 2048), F32),
        ),
        in_specs=[hbm, hbm, hbm],
        out_specs=(hbm, hbm, hbm, hbm),
        scratch_shapes=[
            vmem((16, 20, 16, 128), BF16), vmem((64, 2, 4096), F32), vmem((64, 2048), F32),
            vmem((128, 4096), BF16), vmem((16, 16, 2048), BF16), dma((10,)),
        ],
        compiler_params=pltpu.CompilerParams(vmem_limit_bytes=60 * 2**20),
        name="lay_out",
    )(mid_acts, mid_w, mid_rec)
    return o_acts, o_w.reshape(256, 2048), o_mod, o_gate


def solution(mesh):
    placed = (
        P(("rep", "shard"), None),
        P(("rep", "shard"), None),
        P(("rep", "shard"), None),
        P("shard", None),
        P(),
        P(),
        P(("rep", "shard")),
    )
    return jax.shard_map(
        on_device,
        mesh=mesh,
        in_specs=placed,
        out_specs=(P(("rep", "shard"), None), P("shard", None), P(), P()),
        check_vma=False,
    )
```
